256 devices in a mesh: dp: 4 (over y), expert: 64 (over x, z, core).
Axes of the slice: x: 4, y: 4, z: 8, core: 2. Of those that a mesh axis runs over, the one named last changes fastest.
Arguments:
- tokens: bfloat16 [8192, 3584], P('expert', 'dp'), may hold values from -6 to 6
- cotangent: bfloat16 [8192, 3584], P('expert', 'dp'), may hold values from -6 to 6
- expert_ids: int32 [8192, 4], P('expert'), may hold values from 0 to 55, all different within a row; in each aligned block of 128 rows (0 to 127, 128 to 255, ...) at most 11 rows name the same one
- gate_probs: bfloat16 [8192, 4], P('expert'), may hold values from 0.049804688 to 1
- slot_expert: int32 [64], replicated, may hold values from 0 to 55, as said below
- w_gate: bfloat16 [64, 3584, 1024], P('expert', None, 'dp'), as said below
- w_up: bfloat16 [64, 3584, 1024], P('expert', None, 'dp'), as said below
- w_down: bfloat16 [64, 1024, 3584], P('expert', 'dp'), as said below
Outputs:
- d_tokens: bfloat16 [8192, 3584], P('expert', 'dp')
- d_probs: float32 [8192, 4], P('expert')
- grad_gate: bfloat16 [64, 3584, 1024], P('expert', None, 'dp')
- grad_up: bfloat16 [64, 3584, 1024], P('expert', None, 'dp')
- grad_down: bfloat16 [64, 1024, 3584], P('expert', 'dp')
The draws below stay inside these ranges and needn't reach their ends.
Inputs may be any that keep to these rules, and one draw needn't show every extreme that they name: `expert_ids`: in each aligned block of 128 rows no expert is named by more than 11 rows, a bound that some block reaches. `slot_expert`: every expert appears once or twice; an expert that appears twice holds slots 2 j and 2 j + 1 for some j, and 8 experts appear twice. `w_gate`: slots that hold the same expert hold equal weights. `w_up`: slots that hold the same expert hold equal weights. `w_down`: slots that hold the same expert hold equal weights.
All inputs are finite; a program needn't handle non-finite values.
Results may differ from the reference program's by a relative error of at most 0.015.
Values may be sent and summed in bfloat16 or wider, within the bound.
No kernel may reach another device: no remote copies, remote signals or barrier semaphores. Data moves between devices by JAX's collectives and lax.ppermute only.
A program may use at most 256 MiB of HBM per device.

```python
import math
import jax
import jax.numpy as jnp
import numpy as np
from jax import lax

D = 3584
HID = 1024
TOP = 4
TOK_GRP = 128
REPL = 8
SLOTS = 64
EXPERTS = 56
CAP = 11
TOKENS = 8192
N_DP = 4
N_EXPERT = 64


def placement_table(key):
    order_key, pick_key = jax.random.split(key)
    pair_count = SLOTS // 2
    middle = (jax.random.permutation(pick_key, pair_count - 2) < REPL - 2).astype(jnp.int32)
    marked = jnp.concatenate([jnp.ones((1,), jnp.int32), middle, jnp.ones((1,), jnp.int32)])
    slot_range = jnp.arange(SLOTS, dtype=jnp.int32)
    fresh = 1 - slot_range % 2 * marked[slot_range // 2]
    position = (jnp.cumsum(fresh) - 1).astype(jnp.int32)
    shuffled = jax.random.permutation(order_key, EXPERTS).astype(jnp.int32)
    return shuffled[position]


def draw_slot_expert(key, part):
    return placement_table(key)


def draw_w_gate(key, part):
    table = placement_table(key)
    key = jax.random.fold_in(key, 21)

    def one_slot(expert):
        sub = jax.random.fold_in(key, expert)
        return jax.random.normal(sub, (D, HID), jnp.float32)
    return (jax.vmap(one_slot)(table) * D ** (-0.5)).astype(jnp.bfloat16)


def draw_w_up(key, part):
    table = placement_table(key)
    key = jax.random.fold_in(key, 22)

    def one_slot(expert):
        sub = jax.random.fold_in(key, expert)
        return jax.random.normal(sub, (D, HID), jnp.float32)
    return (jax.vmap(one_slot)(table) * D ** (-0.5)).astype(jnp.bfloat16)


def draw_w_down(key, part):
    table = placement_table(key)
    key = jax.random.fold_in(key, 23)

    def one_slot(expert):
        sub = jax.random.fold_in(key, expert)
        return jax.random.normal(sub, (HID, D), jnp.float32)
    return (jax.vmap(one_slot)(table) * HID ** (-0.5)).astype(jnp.bfloat16)


def shard_levels(stream_key, extent, shards, low, high):
    factor_of = 1.0
    for dim, blocks in shards:
        heights = jax.random.uniform(jax.random.fold_in(jax.random.fold_in(stream_key, 6), dim), (blocks,), jnp.float32, low / len(shards), high / len(shards))
        factor_of = factor_of * jnp.repeat(jnp.exp(heights), extent[dim] // blocks).reshape((-1,) + (1,) * (len(extent) - 1 - dim))
    return factor_of


def shared_out(stream_key, own, number, rows, count, top, reach, skew):
    order = jax.random.permutation(stream_key, count)
    crowded, usual = shares(count, rows * top, reach, skew, True), shares(count, rows * top, reach, skew, False)
    places = jnp.arange(count)

    def named(lengths, offset_by):
        used = int((lengths > 0).sum())
        fixed = max(1, used // 4)
        shifted = fixed + (places - fixed + offset_by * (used - fixed)) % max(1, count - fixed)
        return jnp.zeros((count,), jnp.int32).at[order[jnp.where(places < fixed, places, shifted)]].set(jnp.asarray(lengths, jnp.int32))

    lengths = jnp.where(number % 4 == 0, named(crowded, number // 4), named(usual, number - number // 4 - 1))
    mixed = jax.random.permutation(jax.random.fold_in(own, 3), count)
    giver, receiver = mixed[0:count // 2 * 2:2], mixed[1:count // 2 * 2:2]
    slack = jnp.minimum(lengths[giver] - 1, reach - lengths[receiver]) // 2
    slack = jnp.where((giver == order[0]) | (receiver == order[0]) | (lengths[receiver] == 0), 0, jnp.maximum(slack, 0))
    shifted = jax.random.randint(jax.random.fold_in(own, 4), (count // 2,), 0, 1 << 20) % (slack + 1)
    lengths = lengths.at[giver].add(-shifted).at[receiver].add(shifted)
    labels = jnp.searchsorted(jnp.cumsum(lengths), jnp.arange(rows * top), side="right").astype(jnp.int32)
    listing = labels.reshape(top, rows).T
    listing = listing[jax.random.permutation(jax.random.fold_in(own, 1), rows)]
    offset_by = jax.random.randint(jax.random.fold_in(own, 2), (rows, 1), 0, top)
    return jnp.take_along_axis(listing, (jnp.arange(top)[None, :] + offset_by) % top, axis=1)


def shares(number_of, total, most, skew, full):
    loads = [(1 << 20) // math.isqrt(grade ** skew) + 1 for grade in range(1, number_of + 1)]
    largest = most if full else min(most, max(-(-total // number_of), total * loads[0] // sum(loads)))
    least = 1 if total - largest >= number_of - 1 else 0
    given, rest = [largest] + [least] * (number_of - 1), total - largest - least * (number_of - 1)
    while rest > 0:
        candidates = [i for i in range(1, number_of) if given[i] < largest] or [i for i in range(1, number_of) if given[i] < most]
        mass, left = sum([loads[i] for i in candidates]), rest
        for i in candidates:
            more = min(most - given[i], max(1, left * loads[i] // mass), rest)
            given[i] = given[i] + more
            rest = rest - more
    return np.array(given)


def centred(rng, dims, deviation, bound, cuts=(), kind=jnp.bfloat16):
    drawn = deviation * jax.random.normal(rng, dims, jnp.float32)
    if cuts:
        drawn = drawn * shard_levels(rng, dims, cuts, -0.22, 0.18)
    return jnp.clip(drawn, -bound, bound).astype(kind)


def setup_inputs(seed: int = 0) -> dict:
    splits = jax.random.split(jax.random.key(seed), 9)
    tokens = centred(splits[0], (TOKENS, D), 1.0, 6.0, ((0, 64), (1, 4)))
    cotangent = centred(splits[1], (TOKENS, D), 1.0, 6.0, ((0, 64), (1, 4)))
    expert_ids_keys = jax.random.split(jax.random.fold_in(splits[2], 1), TOKENS // TOK_GRP)
    expert_ids_turns = jax.random.permutation(jax.random.fold_in(splits[2], 3), TOKENS // TOK_GRP)
    expert_ids = jax.vmap(lambda own, number: shared_out(jax.random.fold_in(splits[2], 2), own, number, TOK_GRP, EXPERTS, TOP, CAP, 2))(expert_ids_keys, expert_ids_turns).reshape((TOKENS, TOP))
    gate_probs = jnp.clip(0.049804688 + 0.9501953 * jax.random.uniform(splits[3], (TOKENS, TOP), jnp.float32) ** shard_levels(splits[3], (TOKENS, TOP), ((0, 64),), -0.2, 0.2), 0.049804688, 1.0).astype(jnp.bfloat16)
    slot_expert = draw_slot_expert(jax.random.fold_in(splits[8], 71), 0)
    w_gate = draw_w_gate(jax.random.fold_in(splits[8], 71), 0)
    w_up = draw_w_up(jax.random.fold_in(splits[8], 71), 0)
    w_down = draw_w_down(jax.random.fold_in(splits[8], 71), 0)
    return {"tokens": tokens, "cotangent": cotangent, "expert_ids": expert_ids, "gate_probs": gate_probs, "slot_expert": slot_expert, "w_gate": w_gate, "w_up": w_up, "w_down": w_down}


def silu_parts(gate):
    sig = jax.nn.sigmoid(gate)
    return gate * sig, sig * (1.0 + gate * (1.0 - sig))


def contract(left, right, left_dim, right_dim):
    return lax.dot_general(left, right, (((left_dim,), (right_dim,)), ((), ())), preferred_element_type=jnp.float32)


def reference(tokens, cotangent, expert_ids, gate_probs, slot_expert, w_gate, w_up, w_down):
    assigns = TOKENS * TOP
    most_rows = N_EXPERT * CAP
    block = HID // N_DP
    flat_ids = expert_ids.reshape(assigns)
    x_pad = jnp.concatenate([tokens, jnp.zeros((1, D), tokens.dtype)], axis=0)
    dy_pad = jnp.concatenate([cotangent, jnp.zeros((1, D), cotangent.dtype)], axis=0)
    p_pad = jnp.concatenate([gate_probs.reshape(assigns), jnp.zeros((1,), gate_probs.dtype)], axis=0)

    def one_expert(carry, expert):
        dx_acc, score_acc = carry
        picked = jnp.nonzero(flat_ids == expert, size=most_rows, fill_value=assigns)[0].astype(jnp.int32)
        tok_index = (picked // TOP).astype(jnp.int32)
        xs = x_pad[tok_index]
        dys = dy_pad[tok_index]
        probs = p_pad[picked]
        slot = jnp.argmax((slot_expert == expert).astype(jnp.int32)).astype(jnp.int32)
        wg = w_gate[slot]
        wu = w_up[slot]
        wd = w_down[slot]
        gate = jnp.dot(xs, wg, preferred_element_type=jnp.float32)
        up = jnp.dot(xs, wu, preferred_element_type=jnp.float32)
        act, slope = silu_parts(gate)
        hidden = (act * up).astype(jnp.bfloat16)
        out = jnp.dot(hidden, wd, preferred_element_type=jnp.float32)
        score = jnp.sum(dys.astype(jnp.float32) * out, axis=1)
        d_out = (probs.astype(jnp.float32)[:, None] * dys.astype(jnp.float32)).astype(jnp.bfloat16)
        d_hidden = contract(d_out, wd, 1, 1)
        d_gate_pre = (d_hidden * up * slope).astype(jnp.bfloat16)
        d_up_pre = (d_hidden * act).astype(jnp.bfloat16)
        g_down = contract(hidden, d_out, 0, 0).astype(jnp.bfloat16)
        g_gate = contract(xs, d_gate_pre, 0, 0).astype(jnp.bfloat16)
        g_up = contract(xs, d_up_pre, 0, 0).astype(jnp.bfloat16)
        pieces = jnp.zeros((most_rows, D), jnp.float32)
        for index in range(N_DP):
            lo = index * block
            piece = contract(d_gate_pre[:, lo:lo + block], wg[:, lo:lo + block], 1, 1)
            piece = piece + contract(d_up_pre[:, lo:lo + block], wu[:, lo:lo + block], 1, 1)
            rounded = lax.optimization_barrier(piece.astype(jnp.bfloat16))
            pieces = pieces + rounded.astype(jnp.float32)
        dx_acc = dx_acc.at[tok_index].add(pieces)
        score_acc = score_acc.at[picked].set(score)
        return (dx_acc, score_acc), (g_gate, g_up, g_down)

    start = (jnp.zeros((TOKENS + 1, D), jnp.float32), jnp.zeros((assigns + 1,), jnp.float32))
    (dx_acc, score_acc), (all_gate, all_up, all_down) = lax.scan(one_expert, start, jnp.arange(EXPERTS, dtype=jnp.int32))
    d_tokens = dx_acc[:TOKENS].astype(jnp.bfloat16)
    d_probs = score_acc[:assigns].reshape(TOKENS, TOP)
    return d_tokens, d_probs, all_gate[slot_expert], all_up[slot_expert], all_down[slot_expert]
```

```python
import functools

import jax
import jax.numpy as jnp
from jax import lax
from jax.experimental import pallas as pl
from jax.experimental.pallas import tpu as pltpu
from jax.sharding import PartitionSpec as P

F32 = jnp.float32
BF16 = jnp.bfloat16
SLOTS = 64
CAP = 11
BLOCK = 12
TOK = 128
ROWS = SLOTS * CAP
HALF = ROWS // 2
PADDED = SLOTS * BLOCK
QUARTER = 896
WIDTH = 3584
SHARE = 256
N_DP = 4
TILE = 176
TILES = ROWS // TILE
VMEM = pltpu.VMEM


def iota(shape, dim):
    return lax.broadcasted_iota(jnp.int32, shape, dim)


def dot(left, right, left_dim=1, right_dim=0, precision=None):
    return lax.dot_general(
        left, right, (((left_dim,), (right_dim,)), ((), ())),
        precision=precision, preferred_element_type=F32,
    )


def params(mib):
    return pltpu.CompilerParams(vmem_limit_bytes=mib << 20)


def pack_kernel(parity_ref, slot_ref, ids_ref, probs_ref, tok_ref, cot_ref, x_ref, d_ref, code_ref, pick_ref):
    slot = slot_ref[...]
    index = iota((SLOTS, TOK), 0)
    second = (index & 1).astype(F32)
    partner = jnp.where(second > 0, pltpu.roll(slot, 1, 0), pltpu.roll(slot, SLOTS - 1, 0))
    paired = slot == partner
    ids = ids_ref[...].astype(F32)
    probs = probs_ref[...].astype(F32)
    chosen = jnp.zeros((SLOTS, TOK), F32)
    weight = jnp.zeros((SLOTS, TOK), F32)
    for k in range(4):
        here = slot == ids[k:k + 1, :]
        chosen = chosen + jnp.where(here, 1.0, 0.0)
        weight = weight + jnp.where(here, probs[k:k + 1, :], 0.0)
    earlier = jnp.where(iota((TOK, TOK), 0) < iota((TOK, TOK), 1), 1.0, 0.0).astype(BF16)
    rank = dot(chosen.astype(BF16), earlier)
    shifted = rank + parity_ref[0].astype(F32)
    half = jnp.floor(shifted * 0.5)
    taken = jnp.where(paired, jnp.where(shifted - 2.0 * half == second, 1.0, 0.0), 1.0) * chosen
    place = jnp.where(paired, half, rank)
    code = jnp.where(taken > 0, place + 1.0, 0.0)
    code_ref[...] = code
    row, col = iota((PADDED, SLOTS), 0), iota((PADDED, SLOTS), 1) * BLOCK
    spread = jnp.where(row >= col, jnp.where(row < col + BLOCK, 1.0, 0.0), 0.0).astype(BF16)
    number = iota((PADDED, TOK), 0).astype(F32)
    within = number - BLOCK * jnp.floor((number + 0.5) * (1.0 / BLOCK)) + 1.0
    pick = jnp.where(dot(spread, code.astype(BF16)) == within, 1.0, 0.0)
    scaled = pick * dot(spread, weight.astype(BF16))
    pick = pick.astype(BF16)
    pick_ref[...] = pick
    x_ref[...] = dot(pick, tok_ref[...]).astype(BF16)
    d_ref[...] = dot(scaled.astype(BF16), cot_ref[...]).astype(BF16)


def pack(parity, slot, ids, probs, tokens, cotangent):
    whole = pl.BlockSpec(memory_space=VMEM)
    return pl.pallas_call(
        pack_kernel,
        out_shape=(
            jax.ShapeDtypeStruct((PADDED, QUARTER), BF16),
            jax.ShapeDtypeStruct((PADDED, QUARTER), BF16),
            jax.ShapeDtypeStruct((SLOTS, TOK), F32),
            jax.ShapeDtypeStruct((PADDED, TOK), BF16),
        ),
        in_specs=[pl.BlockSpec(memory_space=pltpu.SMEM)] + [whole] * 5,
        out_specs=(whole,) * 4,
        compiler_params=params(24),
        cost_estimate=pl.CostEstimate(flops=400_000_000, bytes_accessed=4_000_000, transcendentals=0),
    )(parity, slot, ids, probs, tokens, cotangent)


def combine_kernel(slot_ref, ids_ref, probs_ref, code_ref, pick_ref, back_ref, dtok_ref, dprob_ref):
    dtok_ref[...] = dot(pick_ref[...], back_ref[...], 0, 0).astype(BF16)
    chosen = jnp.where(
        iota((SLOTS, PADDED), 1) == iota((SLOTS, PADDED), 0) * BLOCK + CAP, 1.0, 0.0
    ).astype(BF16)
    scores = dot(chosen, back_ref[:, 0:TOK]) + dot(chosen, back_ref[:, TOK:2 * TOK])
    code = code_ref[...]
    placed = jnp.zeros((SLOTS, TOK), F32)
    for r in range(CAP):
        placed = placed + jnp.where(code == r + 1.0, scores[:, r:r + 1], 0.0)
    ids = ids_ref[...].astype(F32)
    probs = probs_ref[...].astype(F32)
    slot = slot_ref[...]
    found = [
        jnp.sum(jnp.where(slot == ids[k:k + 1, :], placed, 0.0), axis=0, keepdims=True)
        for k in range(4)
    ]
    dprob_ref[...] = jnp.concatenate(found, axis=0) / probs


def combine(slot, ids, probs, code, pick, back):
    whole = pl.BlockSpec(memory_space=VMEM)
    return pl.pallas_call(
        combine_kernel,
        out_shape=(
            jax.ShapeDtypeStruct((TOK, QUARTER), BF16),
            jax.ShapeDtypeStruct((4, TOK), F32),
        ),
        in_specs=[whole] * 6,
        out_specs=(whole,) * 2,
        compiler_params=params(24),
        cost_estimate=pl.CostEstimate(flops=200_000_000, bytes_accessed=2_000_000, transcendentals=0),
    )(slot, ids, probs, code, pick, back)


def part_specs():
    full = pl.BlockSpec((TILE, QUARTER), lambda m, at: (m, 0))
    low = pl.BlockSpec((TILE, QUARTER), lambda m, at: (jnp.minimum(m, TILES // 2 - 1), 0))
    high = pl.BlockSpec((TILE, QUARTER), lambda m, at: (jnp.maximum(m - TILES // 2, 0), 0))
    return [full, full, full, low, high]


def offset(at_ref, rel):
    return pl.multiple_of(lax.rem(at_ref[0] + rel, N_DP) * QUARTER, 128)


RELS = (0, 3, 1, 2)


def forward_kernel(at_ref, own, below, above, low, high, wg_ref, wu_ref, hid_ref, act_ref, ups_ref):
    m = pl.program_id(0)
    far = jnp.where(m < TILES // 2, low[...], high[...])
    gate = jnp.zeros((TILE, SHARE), F32)
    up = jnp.zeros((TILE, SHARE), F32)
    for rel, part in zip(RELS, (own[...], below[...], above[...], far)):
        where = pl.ds(offset(at_ref, rel), QUARTER)
        gate = gate + dot(part, wg_ref[where, :])
        up = up + dot(part, wu_ref[where, :])
    sig = jax.nn.sigmoid(gate)
    act = gate * sig
    hid_ref[...] = (act * up).astype(BF16)
    act_ref[...] = act
    ups_ref[...] = up * (sig * (1.0 + gate * (1.0 - sig)))


def forward(at, parts, wg, wu):
    tile = pl.BlockSpec((TILE, SHARE), lambda m, at: (m, 0))
    whole = pl.BlockSpec((WIDTH, SHARE), lambda m, at: (0, 0))
    return pl.pallas_call(
        forward_kernel,
        out_shape=(
            jax.ShapeDtypeStruct((ROWS, SHARE), BF16),
            jax.ShapeDtypeStruct((ROWS, SHARE), F32),
            jax.ShapeDtypeStruct((ROWS, SHARE), F32),
        ),
        grid_spec=pltpu.PrefetchScalarGridSpec(
            num_scalar_prefetch=1, grid=(TILES,),
            in_specs=part_specs() + [whole, whole], out_specs=(tile,) * 3,
        ),
        compiler_params=params(32),
        cost_estimate=pl.CostEstimate(
            flops=4 * ROWS * WIDTH * SHARE, bytes_accessed=11_000_000, transcendentals=ROWS * SHARE
        ),
    )(at, *parts, wg, wu)


def backward_kernel(at_ref, own, below, above, low, high, wd_ref, hid_ref, act_ref, ups_ref, dg_ref, du_ref, score_ref):
    m = pl.program_id(0)
    far = jnp.where(m < TILES // 2, low[...], high[...])
    d_hidden = jnp.zeros((TILE, SHARE), F32)
    for rel, part in zip(RELS, (own[...], below[...], above[...], far)):
        d_hidden = d_hidden + dot(part, wd_ref[:, pl.ds(offset(at_ref, rel), QUARTER)], 1, 1)
    dg_ref[...] = (d_hidden * ups_ref[...]).astype(BF16)
    du_ref[...] = (d_hidden * act_ref[...]).astype(BF16)
    score = jnp.sum(hid_ref[...].astype(F32) * d_hidden, axis=1, keepdims=True)
    slots = TILE // CAP
    number = iota((TILE, TOK), 0).astype(F32)
    within = number - CAP * jnp.floor((number + 0.5) * (1.0 / CAP))
    lanes = jnp.where(iota((TILE, TOK), 1).astype(F32) == within, score, 0.0)
    row, col = iota((slots, TILE), 0) * CAP, iota((slots, TILE), 1)
    group = jnp.where(col >= row, jnp.where(col < row + CAP, 1.0, 0.0), 0.0)
    score_ref[...] = dot(group, lanes, precision=lax.Precision.HIGHEST)


def backward(at, parts, wd, hid, act, ups):
    tile = pl.BlockSpec((TILE, SHARE), lambda m, at: (m, 0))
    whole = pl.BlockSpec((SHARE, WIDTH), lambda m, at: (0, 0))
    return pl.pallas_call(
        backward_kernel,
        out_shape=(
            jax.ShapeDtypeStruct((ROWS, SHARE), BF16),
            jax.ShapeDtypeStruct((ROWS, SHARE), BF16),
            jax.ShapeDtypeStruct((SLOTS, TOK), F32),
        ),
        grid_spec=pltpu.PrefetchScalarGridSpec(
            num_scalar_prefetch=1, grid=(TILES,),
            in_specs=part_specs() + [whole, tile, tile, tile],
            out_specs=(tile, tile, pl.BlockSpec((TILE // CAP, TOK), lambda m, at: (m, 0))),
        ),
        compiler_params=params(32),
        cost_estimate=pl.CostEstimate(
            flops=2 * ROWS * WIDTH * SHARE, bytes_accessed=9_000_000, transcendentals=0
        ),
    )(at, *parts, wd, hid, act, ups)


def piece_kernel(n_add, at_ref, dg_ref, du_ref, wg_ref, wu_ref, *refs):
    out_ref = refs[-1]
    total = dot(dg_ref[...], wg_ref[...], 1, 1) + dot(du_ref[...], wu_ref[...], 1, 1)
    for ref in refs[:n_add]:
        total = total + ref[...].astype(F32)
    out_ref[...] = total.astype(BF16)


def piece(at, rel, first, rows, dg, du, wg, wu, adds=()):
    start = first // TILE
    tile = pl.BlockSpec((TILE, SHARE), lambda m, at: (m + start, 0))
    weight = pl.BlockSpec((QUARTER, SHARE), lambda m, at: (lax.rem(at[0] + rel, N_DP), 0))
    out = pl.BlockSpec((TILE, QUARTER), lambda m, at: (m, 0))
    return pl.pallas_call(
        functools.partial(piece_kernel, len(adds)),
        out_shape=jax.ShapeDtypeStruct((rows, QUARTER), BF16),
        grid_spec=pltpu.PrefetchScalarGridSpec(
            num_scalar_prefetch=1, grid=(rows // TILE,),
            in_specs=[tile, tile, weight, weight] + [out] * len(adds), out_specs=out,
        ),
        compiler_params=params(24),
        cost_estimate=pl.CostEstimate(
            flops=4 * rows * QUARTER * SHARE, bytes_accessed=3_000_000, transcendentals=0
        ),
    )(at, dg, du, wg, wu, *adds)


def grads_kernel(at_ref, x0, x1, x2, x3, x4, d0, d1, d2, d3, d4, dg_ref, du_ref, hid_ref, gg_ref, gu_ref, gd_ref):
    dg, du, hid = dg_ref[...], du_ref[...], hid_ref[...]
    step = 128

    def rows_of(parts, cols):
        if len(parts) == 1:
            return parts[0][:, cols]
        return jnp.concatenate([parts[0][:, cols], parts[1][:, cols]], axis=0)

    for rel, xs, ds in zip(RELS, ((x0,), (x1,), (x2,), (x3, x4)), ((d0,), (d1,), (d2,), (d3, d4))):
        base = offset(at_ref, rel)

        def body(c, _, xs=xs, ds=ds, base=base):
            cols = pl.ds(pl.multiple_of(c * step, step), step)
            to = pl.ds(pl.multiple_of(base + c * step, step), step)
            x = rows_of(xs, cols)
            gg_ref[to, :] = dot(x, dg, 0, 0).astype(BF16)
            gu_ref[to, :] = dot(x, du, 0, 0).astype(BF16)
            gd_ref[:, to] = dot(hid, rows_of(ds, cols), 0, 0).astype(BF16)
            return 0

        lax.fori_loop(0, QUARTER // step, body, 0)


def grads(at, xs, ds, dg, du, hid):
    whole = pl.BlockSpec(memory_space=VMEM)
    return pl.pallas_call(
        grads_kernel,
        out_shape=(
            jax.ShapeDtypeStruct((WIDTH, SHARE), BF16),
            jax.ShapeDtypeStruct((WIDTH, SHARE), BF16),
            jax.ShapeDtypeStruct((SHARE, WIDTH), BF16),
        ),
        in_specs=[pl.BlockSpec(memory_space=pltpu.SMEM)] + [whole] * 13,
        out_specs=(whole,) * 3,
        compiler_params=params(32),
        cost_estimate=pl.CostEstimate(
            flops=6 * ROWS * WIDTH * SHARE, bytes_accessed=17_000_000, transcendentals=0
        ),
    )(at, *xs, *ds, dg, du, hid)


def shift(x, by):
    return lax.ppermute(x, "dp", [(i, (i + by) % N_DP) for i in range(N_DP)])


def swap(x):
    return lax.ppermute(x, "expert", [(i, i ^ 1) for i in range(SLOTS)])


def exchange(rows):
    return lax.all_to_all(
        rows.reshape(SLOTS, 3, 4, QUARTER), "expert", split_axis=0, concat_axis=0, tiled=True
    )


def received(rows):
    return rows.reshape(SLOTS, BLOCK, QUARTER)[:, :CAP].reshape(ROWS, QUARTER)


def gather(rows):
    below, above = shift(rows, 1), shift(rows, -1)
    low, high = shift(below[:HALF], 1), shift(above[HALF:], -1)
    return rows, below, above, low, high


def shards(tokens, cotangent, expert_ids, gate_probs, slot_expert, w_gate, w_up, w_down):
    here = lax.axis_index("expert")
    at = lax.axis_index("dp").reshape(1)
    parity = (here % 2).reshape(1)
    wg, wu, wd = w_gate[0], w_up[0], w_down[0]
    ids, probs = expert_ids.T, gate_probs.T
    slot = jnp.broadcast_to(slot_expert.astype(F32)[:, None], (SLOTS, TOK))
    x_rows, d_rows, code, pick = pack(parity, slot, ids, probs, tokens, cotangent)
    xs = gather(received(exchange(x_rows)))
    ds = gather(received(exchange(d_rows)))
    hid, act, ups = forward(at, xs, wg, wu)
    dg, du, score = backward(at, ds, wd, hid, act, ups)

    term = functools.partial(piece, at, dg=dg, du=du, wg=wg, wu=wu)
    far_up = shift(term(2, 0, HALF), 1)
    far_down = shift(term(2, HALF, HALF), -1)
    near_up = shift(term(1, HALF, HALF), 1)
    near_down = shift(term(3, 0, HALF), -1)
    last_up = shift(term(1, 0, HALF, adds=(far_up,)), 1)
    last_down = shift(term(3, HALF, HALF, adds=(far_down,)), -1)
    total = jnp.concatenate(
        [
            term(0, 0, HALF, adds=(near_down, last_up)),
            term(0, HALF, HALF, adds=(near_up, last_down)),
        ],
        axis=0,
    )
    score = (score + shift(score, 2)) + (shift(score, 1) + shift(score, -1))
    high = lax.reduce_precision(score, 8, 7)
    tail = jnp.concatenate(
        [high, score - high, jnp.zeros((SLOTS, QUARTER - 2 * TOK), F32)], axis=1
    ).astype(BF16)
    pay = jnp.concatenate([total.reshape(SLOTS, CAP, QUARTER), tail[:, None, :]], axis=1)
    back = exchange(pay).reshape(PADDED, QUARTER)
    d_tokens, d_probs = combine(slot, ids, probs, code, pick, back)

    gg, gu, gd = grads(at, xs, ds, dg, du, hid)
    same = slot_expert[here] == slot_expert[here ^ 1]

    def joined(own):
        other = swap(own)
        both = own.astype(F32) + other.astype(F32)
        return jnp.where(same, both, own.astype(F32)).astype(BF16)[None]

    return d_tokens, d_probs.T, joined(gg), joined(gu), joined(gd)


def solution(mesh):
    placed = (
        P("expert", "dp"),
        P("expert", "dp"),
        P("expert", None),
        P("expert", None),
        P(),
        P("expert", None, "dp"),
        P("expert", None, "dp"),
        P("expert", "dp", None),
    )
    return jax.shard_map(
        shards,
        mesh=mesh,
        in_specs=placed,
        out_specs=(
            P("expert", "dp"),
            P("expert", None),
            P("expert", None, "dp"),
            P("expert", None, "dp"),
            P("expert", "dp", None),
        ),
        check_vma=False,
    )
```

```python
import functools

import jax
import jax.numpy as jnp
from jax import lax
from jax.experimental import pallas as pl
from jax.experimental.pallas import tpu as pltpu
from jax.sharding import PartitionSpec as P

F32 = jnp.float32
BF16 = jnp.bfloat16
SLOTS = 64
CAP = 11
BLOCK = 12
TOK = 128
PADDED = SLOTS * BLOCK
HALF = PADDED // 2
QUARTER = 896
WIDTH = 3584
SHARE = 256
N_DP = 4
TILE = 192
TILES = PADDED // TILE
VMEM = pltpu.VMEM
HEAVY = 40_000_000_000


def iota(shape, dim):
    return lax.broadcasted_iota(jnp.int32, shape, dim)


def dot(left, right, left_dim=1, right_dim=0, precision=None):
    return lax.dot_general(
        left, right, (((left_dim,), (right_dim,)), ((), ())),
        precision=precision, preferred_element_type=F32,
    )


def params(mib):
    return pltpu.CompilerParams(vmem_limit_bytes=mib << 20)


def pack_kernel(parity_ref, slot_ref, ids_ref, probs_ref, tok_ref, x_ref, code_ref, pick_ref, scaled_ref):
    slot = slot_ref[...]
    index = iota((SLOTS, TOK), 0)
    second = (index & 1).astype(F32)
    partner = jnp.where(second > 0, pltpu.roll(slot, 1, 0), pltpu.roll(slot, SLOTS - 1, 0))
    paired = slot == partner
    ids = ids_ref[...].astype(F32)
    probs = probs_ref[...].astype(F32)
    chosen = jnp.zeros((SLOTS, TOK), F32)
    weight = jnp.zeros((SLOTS, TOK), F32)
    for k in range(4):
        here = slot == ids[k:k + 1, :]
        chosen = chosen + jnp.where(here, 1.0, 0.0)
        weight = weight + jnp.where(here, probs[k:k + 1, :], 0.0)
    earlier = jnp.where(iota((TOK, TOK), 0) < iota((TOK, TOK), 1), 1.0, 0.0).astype(BF16)
    rank = dot(chosen.astype(BF16), earlier)
    shifted = rank + parity_ref[0].astype(F32)
    half = jnp.floor(shifted * 0.5)
    taken = jnp.where(paired, jnp.where(shifted - 2.0 * half == second, 1.0, 0.0), 1.0) * chosen
    place = jnp.where(paired, half, rank)
    code = jnp.where(taken > 0, place + 1.0, 0.0)
    code_ref[...] = code
    row, col = iota((PADDED, SLOTS), 0), iota((PADDED, SLOTS), 1) * BLOCK
    spread = jnp.where(row >= col, jnp.where(row < col + BLOCK, 1.0, 0.0), 0.0).astype(BF16)
    number = iota((PADDED, TOK), 0).astype(F32)
    within = number - BLOCK * jnp.floor((number + 0.5) * (1.0 / BLOCK)) + 1.0
    pick = jnp.where(dot(spread, code.astype(BF16)) == within, 1.0, 0.0)
    scaled = pick * dot(spread, weight.astype(BF16))
    pick = pick.astype(BF16)
    pick_ref[...] = pick
    scaled_ref[...] = scaled.astype(BF16)
    x_ref[...] = dot(pick, tok_ref[...]).astype(BF16)


def pack(parity, slot, ids, probs, tokens):
    whole = pl.BlockSpec(memory_space=VMEM)
    return pl.pallas_call(
        pack_kernel,
        out_shape=(
            jax.ShapeDtypeStruct((PADDED, QUARTER), BF16),
            jax.ShapeDtypeStruct((SLOTS, TOK), F32),
            jax.ShapeDtypeStruct((PADDED, TOK), BF16),
            jax.ShapeDtypeStruct((PADDED, TOK), BF16),
        ),
        in_specs=[pl.BlockSpec(memory_space=pltpu.SMEM)] + [whole] * 4,
        out_specs=(whole,) * 4,
        compiler_params=params(24),
        cost_estimate=pl.CostEstimate(flops=HEAVY, bytes_accessed=3_000_000, transcendentals=0),
    )(parity, slot, ids, probs, tokens)


def scale_kernel(scaled_ref, cot_ref, out_ref):
    out_ref[...] = dot(scaled_ref[...], cot_ref[...]).astype(BF16)


def scale(scaled, cotangent):
    whole = pl.BlockSpec(memory_space=VMEM)
    return pl.pallas_call(
        scale_kernel,
        out_shape=jax.ShapeDtypeStruct((PADDED, QUARTER), BF16),
        in_specs=[whole] * 2,
        out_specs=whole,
        compiler_params=params(16),
        cost_estimate=pl.CostEstimate(flops=HEAVY, bytes_accessed=2_000_000, transcendentals=0),
    )(scaled, cotangent)


def combine_kernel(slot_ref, ids_ref, probs_ref, code_ref, pick_ref, back_ref, dtok_ref, dprob_ref):
    dtok_ref[...] = dot(pick_ref[...], back_ref[...], 0, 0).astype(BF16)
    chosen = jnp.where(
        iota((SLOTS, PADDED), 1) == iota((SLOTS, PADDED), 0) * BLOCK + CAP, 1.0, 0.0
    ).astype(BF16)
    scores = dot(chosen, back_ref[:, 0:TOK]) + dot(chosen, back_ref[:, TOK:2 * TOK])
    code = code_ref[...]
    placed = jnp.zeros((SLOTS, TOK), F32)
    for r in range(CAP):
        placed = placed + jnp.where(code == r + 1.0, scores[:, r:r + 1], 0.0)
    ids = ids_ref[...].astype(F32)
    probs = probs_ref[...].astype(F32)
    slot = slot_ref[...]
    found = [
        jnp.sum(jnp.where(slot == ids[k:k + 1, :], placed, 0.0), axis=0, keepdims=True)
        for k in range(4)
    ]
    dprob_ref[...] = jnp.concatenate(found, axis=0) / probs


def combine(slot, ids, probs, code, pick, back):
    whole = pl.BlockSpec(memory_space=VMEM)
    return pl.pallas_call(
        combine_kernel,
        out_shape=(
            jax.ShapeDtypeStruct((TOK, QUARTER), BF16),
            jax.ShapeDtypeStruct((4, TOK), F32),
        ),
        in_specs=[whole] * 6,
        out_specs=(whole,) * 2,
        compiler_params=params(24),
        cost_estimate=pl.CostEstimate(flops=200_000_000, bytes_accessed=2_000_000, transcendentals=0),
    )(slot, ids, probs, code, pick, back)


def half_specs(cols):
    low = pl.BlockSpec((TILE, cols), lambda m, at: (jnp.minimum(m, TILES // 2 - 1), 0))
    high = pl.BlockSpec((TILE, cols), lambda m, at: (jnp.maximum(m - TILES // 2, 0), 0))
    return [low, high]


def this_tile(refs):
    lower = pl.program_id(0) < TILES // 2
    return [jnp.where(lower, low[...], high[...]) for low, high in zip(refs[0::2], refs[1::2])]


def offset(at_ref, rel):
    return pl.multiple_of(lax.rem(at_ref[0] + rel, N_DP) * QUARTER, 128)


def weights_kernel(at_ref, wg_ref, wu_ref, wd_ref, *refs):
    for b, out in zip((1, 2, 3), refs):
        where = pl.ds(offset(at_ref, b), QUARTER)
        out[:QUARTER, :] = wg_ref[where, :]
        out[QUARTER:2 * QUARTER, :] = wu_ref[where, :]
        out[2 * QUARTER:, :] = wd_ref[:, where].T


def weights(at, wg, wu, wd):
    whole = pl.BlockSpec(memory_space=VMEM)
    return pl.pallas_call(
        weights_kernel,
        out_shape=(jax.ShapeDtypeStruct((3 * QUARTER, SHARE), BF16),) * 3,
        in_specs=[pl.BlockSpec(memory_space=pltpu.SMEM), whole, whole, whole],
        out_specs=(whole,) * 3,
        compiler_params=params(24),
        cost_estimate=pl.CostEstimate(flops=0, bytes_accessed=9_600_000, transcendentals=0),
    )(at, wg, wu, wd)


def halves_kernel(rows_ref, a1, a2, a3, a4, low_ref, high_ref):
    low_ref[...] = rows_ref[:HALF, :]
    high_ref[...] = rows_ref[HALF:, :]


def halves(rows, after):
    whole = pl.BlockSpec(memory_space=VMEM)
    return pl.pallas_call(
        halves_kernel,
        out_shape=(jax.ShapeDtypeStruct((HALF, QUARTER), BF16),) * 2,
        in_specs=[whole] + [pl.BlockSpec(memory_space=pl.ANY)] * 4,
        out_specs=(whole,) * 2,
        compiler_params=params(16),
        cost_estimate=pl.CostEstimate(flops=HEAVY, bytes_accessed=2_800_000, transcendentals=0),
    )(rows, *after)


def near_kernel(at_ref, *refs):
    wg_ref, wu_ref, out_ref = refs[6:]
    gate = jnp.zeros((TILE, SHARE), F32)
    up = jnp.zeros((TILE, SHARE), F32)
    for rel, part in zip((0, 3, 1), this_tile(refs[:6])):
        where = pl.ds(offset(at_ref, rel), QUARTER)
        gate = gate + dot(part, wg_ref[where, :])
        up = up + dot(part, wu_ref[where, :])
    out_ref[:, :SHARE] = gate
    out_ref[:, SHARE:] = up


def near(at, parts, wg, wu):
    whole = pl.BlockSpec((WIDTH, SHARE), lambda m, at: (0, 0))
    return pl.pallas_call(
        near_kernel,
        out_shape=jax.ShapeDtypeStruct((PADDED, 2 * SHARE), F32),
        grid_spec=pltpu.PrefetchScalarGridSpec(
            num_scalar_prefetch=1, grid=(TILES,),
            in_specs=half_specs(QUARTER) * 3 + [whole, whole],
            out_specs=pl.BlockSpec((TILE, 2 * SHARE), lambda m, at: (m, 0)),
        ),
        compiler_params=params(32),
        cost_estimate=pl.CostEstimate(
            flops=3 * PADDED * WIDTH * SHARE, bytes_accessed=9_000_000, transcendentals=0
        ),
    )(at, *parts, wg, wu)


def forward_kernel(at_ref, low, high, sum_ref, wg_ref, wu_ref, hid_ref, act_ref, ups_ref):
    part = this_tile((low, high))[0]
    gate = sum_ref[:, :SHARE] + dot(part, wg_ref[...])
    up = sum_ref[:, SHARE:] + dot(part, wu_ref[...])
    sig = jax.nn.sigmoid(gate)
    act = gate * sig
    hid_ref[...] = (act * up).astype(BF16)
    act_ref[...] = act
    ups_ref[...] = up * (sig * (1.0 + gate * (1.0 - sig)))


def forward(at, far, summed, wg, wu):
    tile = pl.BlockSpec((TILE, SHARE), lambda m, at: (m, 0))
    rows = pl.BlockSpec((QUARTER, SHARE), lambda m, at: (lax.rem(at[0] + 2, N_DP), 0))
    return pl.pallas_call(
        forward_kernel,
        out_shape=(
            jax.ShapeDtypeStruct((PADDED, SHARE), BF16),
            jax.ShapeDtypeStruct((PADDED, SHARE), F32),
            jax.ShapeDtypeStruct((PADDED, SHARE), F32),
        ),
        grid_spec=pltpu.PrefetchScalarGridSpec(
            num_scalar_prefetch=1, grid=(TILES,),
            in_specs=half_specs(QUARTER)
            + [pl.BlockSpec((TILE, 2 * SHARE), lambda m, at: (m, 0)), rows, rows],
            out_specs=(tile,) * 3,
        ),
        compiler_params=params(32),
        cost_estimate=pl.CostEstimate(
            flops=PADDED * WIDTH * SHARE, bytes_accessed=4_000_000, transcendentals=PADDED * SHARE
        ),
    )(at, *far, summed, wg, wu)


def terms_kernel(at_ref, rows_ref, w0, w1, w2, w3, own_ref, p1, p2, p3):
    rows = rows_ref[...]
    own_ref[...] = dot(rows, w0[...], 1, 1)
    for w, p in ((w1, p1), (w2, p2), (w3, p3)):
        p[...] = dot(rows, w[...]).astype(BF16)


def terms(at, rows, wd, blocks):
    tile = pl.BlockSpec((TILE, SHARE), lambda m, at: (m, 0))
    down = pl.BlockSpec((QUARTER, SHARE), lambda m, at: (2, 0))
    sent = jax.ShapeDtypeStruct((PADDED, SHARE), BF16)
    return pl.pallas_call(
        terms_kernel,
        out_shape=(jax.ShapeDtypeStruct((PADDED, SHARE), F32), sent, sent, sent),
        grid_spec=pltpu.PrefetchScalarGridSpec(
            num_scalar_prefetch=1, grid=(TILES,),
            in_specs=[
                pl.BlockSpec((TILE, QUARTER), lambda m, at: (m, 0)),
                pl.BlockSpec((SHARE, QUARTER), lambda m, at: (0, at[0])),
                down, down, down,
            ],
            out_specs=(tile,) * 4,
        ),
        compiler_params=params(32),
        cost_estimate=pl.CostEstimate(
            flops=2 * PADDED * WIDTH * SHARE, bytes_accessed=5_000_000, transcendentals=0
        ),
    )(at, rows, wd, *blocks)


def within_block(shape):
    number = iota(shape, 0).astype(F32)
    return number - BLOCK * jnp.floor((number + 0.5) * (1.0 / BLOCK))


def slopes_kernel(own, r1, r2, r3, hid_ref, act_ref, ups_ref, low_ref, high_ref):
    d_hidden = own[...] + r1[...].astype(F32) + r2[...].astype(F32) + r3[...].astype(F32)
    dg = d_hidden * ups_ref[...]
    du = d_hidden * act_ref[...]
    score = jnp.sum(hid_ref[...].astype(F32) * d_hidden, axis=1, keepdims=True)
    lanes = jnp.where(iota((TILE, TOK), 1).astype(F32) == within_block((TILE, TOK)), score, 0.0)
    high = lanes.astype(BF16)
    rest = (lanes - high.astype(F32)).astype(BF16)
    row = iota((TILE, TILE), 0).astype(F32)
    start = row - within_block((TILE, TILE))
    col = iota((TILE, TILE), 1).astype(F32)
    spare = within_block((TILE, SHARE)) == CAP
    group = jnp.where(col >= start, jnp.where(col < start + BLOCK, 1.0, 0.0), 0.0).astype(BF16)
    moved = jnp.concatenate([dot(group, high), dot(group, rest)], axis=1)
    both = jnp.concatenate([jnp.where(spare, moved, dg), du], axis=1).astype(BF16)
    m = pl.program_id(0)

    @pl.when(m < TILES // 2)
    def _():
        low_ref[...] = both

    @pl.when(m >= TILES // 2)
    def _():
        high_ref[...] = both


def slopes(own, others, hid, act, ups):
    tile = pl.BlockSpec((TILE, SHARE), lambda m: (m, 0))
    return pl.pallas_call(
        slopes_kernel,
        out_shape=(jax.ShapeDtypeStruct((HALF, 2 * SHARE), BF16),) * 2,
        grid=(TILES,),
        in_specs=[tile] * 7,
        out_specs=(
            pl.BlockSpec((TILE, 2 * SHARE), lambda m: (jnp.minimum(m, TILES // 2 - 1), 0)),
            pl.BlockSpec((TILE, 2 * SHARE), lambda m: (jnp.maximum(m - TILES // 2, 0), 0)),
        ),
        compiler_params=params(24),
        cost_estimate=pl.CostEstimate(flops=50_000_000, bytes_accessed=5_000_000, transcendentals=0),
    )(own, *others, hid, act, ups)


def product(slope, blocks):
    return dot(slope[:, :SHARE], blocks[0], 1, 1) + dot(slope[:, SHARE:], blocks[1], 1, 1)


def back_near_kernel(at_ref, *refs):
    wg_ref, wu_ref, g1, g3, out_ref = refs[6:]
    own, below, above = this_tile(refs[:6])
    total = product(own, (wg_ref[...], wu_ref[...]))
    for slope, g in ((below, g1), (above, g3)):
        total = total + product(slope, (g[:QUARTER, :], g[QUARTER:, :]))
    out_ref[...] = total


def back_kernel(at_ref, *refs):
    sum_ref, g2, out_ref = refs[8:]
    own, below, above, far = this_tile(refs[:8])
    total = sum_ref[...] + product(far, (g2[:QUARTER, :], g2[QUARTER:, :]))
    out_ref[...] = total.astype(BF16)
    parts = [s[:, :SHARE].astype(F32) for s in (own, below, above, far)]
    lanes = (parts[0] + parts[3]) + (parts[1] + parts[2])
    score = lanes[:, :TOK] + lanes[:, TOK:]
    high = score.astype(BF16)
    rest = (score - high.astype(F32)).astype(BF16)
    spare = within_block((TILE, TOK)) == CAP
    out_ref[:, :TOK] = jnp.where(spare, high.astype(F32), total[:, :TOK]).astype(BF16)
    out_ref[:, TOK:2 * TOK] = jnp.where(spare, rest.astype(F32), total[:, TOK:2 * TOK]).astype(BF16)


def back_near(at, parts, wg, wu, blocks):
    mine = pl.BlockSpec((QUARTER, SHARE), lambda m, at: (at[0], 0))
    both = pl.BlockSpec((2 * QUARTER, SHARE), lambda m, at: (0, 0))
    return pl.pallas_call(
        back_near_kernel,
        out_shape=jax.ShapeDtypeStruct((PADDED, QUARTER), F32),
        grid_spec=pltpu.PrefetchScalarGridSpec(
            num_scalar_prefetch=1, grid=(TILES,),
            in_specs=half_specs(2 * SHARE) * 3 + [mine, mine, both, both],
            out_specs=pl.BlockSpec((TILE, QUARTER), lambda m, at: (m, 0)),
        ),
        compiler_params=params(32),
        cost_estimate=pl.CostEstimate(
            flops=3 * PADDED * WIDTH * SHARE, bytes_accessed=8_000_000, transcendentals=0
        ),
    )(at, *parts, wg, wu, blocks[0], blocks[2])


def back_rows(at, parts, summed, block):
    both = pl.BlockSpec((2 * QUARTER, SHARE), lambda m, at: (0, 0))
    tile = pl.BlockSpec((TILE, QUARTER), lambda m, at: (m, 0))
    return pl.pallas_call(
        back_kernel,
        out_shape=jax.ShapeDtypeStruct((PADDED, QUARTER), BF16),
        grid_spec=pltpu.PrefetchScalarGridSpec(
            num_scalar_prefetch=1, grid=(TILES,),
            in_specs=half_specs(2 * SHARE) * 4 + [tile, both], out_specs=tile,
        ),
        compiler_params=params(32),
        cost_estimate=pl.CostEstimate(
            flops=PADDED * WIDTH * SHARE, bytes_accessed=8_000_000, transcendentals=0
        ),
    )(at, *parts, summed, block)


def turn_kernel(*refs):
    half = len(refs) // 3 * 2
    for i, out in enumerate(refs[half:]):
        for c in range(QUARTER // TOK):
            cols = slice(c * TOK, (c + 1) * TOK)
            out[cols, :HALF] = refs[2 * i][:, cols].T
            out[cols, HALF:] = refs[2 * i + 1][:, cols].T


def turn(parts):
    whole = pl.BlockSpec(memory_space=VMEM)
    n = len(parts) // 2
    return pl.pallas_call(
        turn_kernel,
        out_shape=(jax.ShapeDtypeStruct((QUARTER, PADDED), BF16),) * n,
        in_specs=[whole] * (2 * n),
        out_specs=(whole,) * n,
        compiler_params=params(24),
        cost_estimate=pl.CostEstimate(flops=0, bytes_accessed=3_000_000 * n, transcendentals=0),
    )(*parts)


def grads_kernel(at_ref, x0, x1, x2, x3, low_ref, high_ref, gg_ref, gu_ref):
    slope = jnp.concatenate([low_ref[...], high_ref[...]], axis=0)
    step = QUARTER // 4
    for rel, x in zip((0, 3, 1, 2), (x0, x1, x2, x3)):
        base = offset(at_ref, rel)

        def body(c, _, x=x, base=base):
            grad = dot(x[pl.ds(pl.multiple_of(c * step, 32), step), :], slope).astype(BF16)
            to = pl.ds(pl.multiple_of(base + c * step, 32), step)
            gg_ref[to, :] = grad[:, :SHARE]
            gu_ref[to, :] = grad[:, SHARE:]
            return 0

        lax.fori_loop(0, 4, body, 0)


def grads(at, xs, slope):
    whole = pl.BlockSpec(memory_space=VMEM)
    return pl.pallas_call(
        grads_kernel,
        out_shape=(jax.ShapeDtypeStruct((WIDTH, SHARE), BF16),) * 2,
        in_specs=[pl.BlockSpec(memory_space=pltpu.SMEM)] + [whole] * 6,
        out_specs=(whole,) * 2,
        compiler_params=params(32),
        cost_estimate=pl.CostEstimate(
            flops=4 * PADDED * WIDTH * SHARE, bytes_accessed=11_000_000, transcendentals=0
        ),
    )(at, *xs, *slope)


def down_kernel(h0, h1, h2, h3, rows_ref, out_ref):
    for b, h in enumerate((h0, h1, h2, h3)):
        out_ref[b * SHARE:(b + 1) * SHARE, :] = dot(h[...], rows_ref[...], 0, 0).astype(BF16)


def down_grads(hids, rows):
    whole = pl.BlockSpec(memory_space=VMEM)
    return pl.pallas_call(
        down_kernel,
        out_shape=jax.ShapeDtypeStruct((N_DP * SHARE, QUARTER), BF16),
        in_specs=[whole] * 5,
        out_specs=whole,
        compiler_params=params(24),
        cost_estimate=pl.CostEstimate(
            flops=HEAVY, bytes_accessed=5_000_000, transcendentals=0
        ),
    )(*hids, rows)


def join_kernel(n_out, same_ref, mine_ref, other_ref, *outs):
    mine = mine_ref[...].astype(F32)
    both = jnp.where(same_ref[0] > 0, mine + other_ref[...].astype(F32), mine).astype(BF16)
    rows = both.shape[0] // n_out
    for b, out in enumerate(outs):
        out[...] = both[b * rows:(b + 1) * rows]


def join(same, mine, other, n_out):
    rows, cols = mine.shape
    steps = 7 if n_out == 1 else 1
    block = pl.BlockSpec((rows // steps, cols), lambda m, same: (m, 0))
    out = pl.BlockSpec((rows // steps // n_out, cols), lambda m, same: (m, 0))
    return pl.pallas_call(
        functools.partial(join_kernel, n_out),
        out_shape=(jax.ShapeDtypeStruct((rows // n_out, cols), BF16),) * n_out,
        grid_spec=pltpu.PrefetchScalarGridSpec(
            num_scalar_prefetch=1, grid=(steps,),
            in_specs=[block, block], out_specs=(out,) * n_out,
        ),
        compiler_params=params(24),
        cost_estimate=pl.CostEstimate(flops=0, bytes_accessed=0, transcendentals=0),
    )(same, mine, other)


def place_kernel(at_ref, p0, p1, p2, p3, out_ref):
    for rel, p in enumerate((p0, p1, p2, p3)):
        out_ref[:, pl.ds(offset(at_ref, rel), QUARTER)] = p[...]


def placed(at, parts):
    whole = pl.BlockSpec(memory_space=VMEM)
    return pl.pallas_call(
        place_kernel,
        out_shape=jax.ShapeDtypeStruct((SHARE, WIDTH), BF16),
        in_specs=[pl.BlockSpec(memory_space=pltpu.SMEM)] + [whole] * 4,
        out_specs=whole,
        compiler_params=params(16),
        cost_estimate=pl.CostEstimate(flops=0, bytes_accessed=0, transcendentals=0),
    )(at, *parts)


def shift(x, by):
    return lax.ppermute(x, "dp", [(i, (i + by) % N_DP) for i in range(N_DP)])


def swap(x):
    return lax.ppermute(x, "expert", [(i, i ^ 1) for i in range(SLOTS)])


def exchange(rows):
    return lax.all_to_all(
        rows.reshape(SLOTS, 3, 4, QUARTER), "expert", split_axis=0, concat_axis=0, tiled=True
    )


def ring(low, high):
    low_below, high_above = shift(low, 1), shift(high, -1)
    high_below, low_above = shift(high, 1), shift(low, -1)
    far = [shift(low_below, 1), shift(high_above, -1)]
    return [low, high], [low_below, high_below], [low_above, high_above], far


def ordered(arrays):
    return lax.optimization_barrier(arrays)


def shards(tokens, cotangent, expert_ids, gate_probs, slot_expert, w_gate, w_up, w_down):
    here = lax.axis_index("expert")
    at = lax.axis_index("dp").reshape(1)
    parity = (here % 2).reshape(1)
    wg, wu, wd = w_gate[0], w_up[0], w_down[0]
    ids, probs = expert_ids.T, gate_probs.T
    slot = jnp.broadcast_to(slot_expert.astype(F32)[:, None], (SLOTS, TOK))
    x_rows, code, pick, scaled = pack(parity, slot, ids, probs, tokens)
    d_rows = scale(scaled, cotangent)
    sent = weights(at, wg, wu, wd)
    blocks = [shift(w, b) for w, b in zip(sent, (1, 2, 3))]
    x_rows, token = ordered((x_rows, swap(sent[0][:16])))
    x_here = exchange(x_rows).reshape(PADDED, QUARTER)
    x_own, x_below, x_above, x_far = ring(*halves(x_here, (*blocks, token)))
    d_here, x_below, x_above = ordered((exchange(d_rows), x_below, x_above))
    d_here = d_here.reshape(PADDED, QUARTER)

    own, *out = terms(at, d_here, wd, blocks)
    others = [shift(out[b - 1], -b) for b in (2, 1, 3)]
    x_parts, own = ordered((x_own + x_below + x_above, own))
    x_turned = turn(x_parts)
    x_far, x_turned = ordered((x_far, x_turned))
    hid, act, ups = forward(at, x_far, near(at, x_parts, wg, wu), wg, wu)
    s_own, s_below, s_above, s_far = ring(*slopes(own, others, hid, act, ups))
    s_far, far_turned = ordered((s_far, turn(ordered((x_far, hid))[0])))
    summed = back_near(at, s_own + s_below + s_above, wg, wu, blocks)
    pay = back_rows(at, s_own + s_below + s_above + s_far, summed, blocks[1])
    back = exchange(pay).reshape(PADDED, QUARTER)
    d_tokens, d_probs = combine(slot, ids, probs, code, pick, back)

    same = (slot_expert[here] == slot_expert[here ^ 1]).astype(jnp.int32).reshape(1)
    hid = ordered((hid, s_below))[0]
    gg, gu = grads(at, x_turned + far_turned, ordered((s_own, pay))[0])
    gd = down_grads([hid] + [shift(hid, b) for b in (1, 2, 3)], d_here)
    pieces = join(same, gd, swap(gd), N_DP)
    grad_down = placed(at, [pieces[0]] + [shift(pieces[b], -b) for b in (1, 2, 3)])
    grad_gate = join(same, gg, swap(gg), 1)[0]
    grad_up = join(same, gu, swap(gu), 1)[0]
    return d_tokens, d_probs.T, grad_gate[None], grad_up[None], grad_down[None]


def solution(mesh):
    specs = (
        P("expert", "dp"),
        P("expert", "dp"),
        P("expert", None),
        P("expert", None),
        P(),
        P("expert", None, "dp"),
        P("expert", None, "dp"),
        P("expert", "dp", None),
    )
    return jax.shard_map(
        shards,
        mesh=mesh,
        in_specs=specs,
        out_specs=(
            P("expert", "dp"),
            P("expert", None),
            P("expert", None, "dp"),
            P("expert", None, "dp"),
            P("expert", "dp", None),
        ),
        check_vma=False,
    )
```

```python
import functools

import jax
import jax.numpy as jnp
from jax import lax
from jax.experimental import pallas as pl
from jax.experimental.pallas import tpu as pltpu
from jax.sharding import PartitionSpec as P

F32 = jnp.float32
BF16 = jnp.bfloat16
SLOTS = 64
CAP = 11
BLOCK = 12
TOK = 128
PADDED = SLOTS * BLOCK
HALF = PADDED // 2
QUARTER = 896
WIDTH = 3584
SHARE = 256
N_DP = 4
TILE = 192
TILES = PADDED // TILE
VMEM = pltpu.VMEM
HEAVY = 40_000_000_000


def iota(shape, dim):
    return lax.broadcasted_iota(jnp.int32, shape, dim)


def dot(left, right, left_dim=1, right_dim=0, precision=None):
    return lax.dot_general(
        left, right, (((left_dim,), (right_dim,)), ((), ())),
        precision=precision, preferred_element_type=F32,
    )


def params(mib):
    return pltpu.CompilerParams(vmem_limit_bytes=mib << 20)


def pack_kernel(parity_ref, slot_ref, ids_ref, probs_ref, tok_ref, x_ref, code_ref, pick_ref, scaled_ref):
    slot = slot_ref[...]
    index = iota((SLOTS, TOK), 0)
    second = (index & 1).astype(F32)
    partner = jnp.where(second > 0, pltpu.roll(slot, 1, 0), pltpu.roll(slot, SLOTS - 1, 0))
    paired = slot == partner
    ids = ids_ref[...].astype(F32)
    probs = probs_ref[...].astype(F32)
    chosen = jnp.zeros((SLOTS, TOK), F32)
    weight = jnp.zeros((SLOTS, TOK), F32)
    for k in range(4):
        here = slot == ids[k:k + 1, :]
        chosen = chosen + jnp.where(here, 1.0, 0.0)
        weight = weight + jnp.where(here, probs[k:k + 1, :], 0.0)
    earlier = jnp.where(iota((TOK, TOK), 0) < iota((TOK, TOK), 1), 1.0, 0.0).astype(BF16)
    rank = dot(chosen.astype(BF16), earlier)
    shifted = rank + parity_ref[0].astype(F32)
    half = jnp.floor(shifted * 0.5)
    taken = jnp.where(paired, jnp.where(shifted - 2.0 * half == second, 1.0, 0.0), 1.0) * chosen
    place = jnp.where(paired, half, rank)
    code = jnp.where(taken > 0, place + 1.0, 0.0)
    code_ref[...] = code
    row, col = iota((PADDED, SLOTS), 0), iota((PADDED, SLOTS), 1) * BLOCK
    spread = jnp.where(row >= col, jnp.where(row < col + BLOCK, 1.0, 0.0), 0.0).astype(BF16)
    number = iota((PADDED, TOK), 0).astype(F32)
    within = number - BLOCK * jnp.floor((number + 0.5) * (1.0 / BLOCK)) + 1.0
    pick = jnp.where(dot(spread, code.astype(BF16)) == within, 1.0, 0.0)
    scaled = pick * dot(spread, weight.astype(BF16))
    pick = pick.astype(BF16)
    pick_ref[...] = pick
    scaled_ref[...] = scaled.astype(BF16)
    x_ref[...] = dot(pick, tok_ref[...]).astype(BF16)


def pack(parity, slot, ids, probs, tokens):
    whole = pl.BlockSpec(memory_space=VMEM)
    return pl.pallas_call(
        pack_kernel,
        out_shape=(
            jax.ShapeDtypeStruct((PADDED, QUARTER), BF16),
            jax.ShapeDtypeStruct((SLOTS, TOK), F32),
            jax.ShapeDtypeStruct((PADDED, TOK), BF16),
            jax.ShapeDtypeStruct((PADDED, TOK), BF16),
        ),
        in_specs=[pl.BlockSpec(memory_space=pltpu.SMEM)] + [whole] * 4,
        out_specs=(whole,) * 4,
        compiler_params=params(24),
        cost_estimate=pl.CostEstimate(flops=HEAVY, bytes_accessed=3_000_000, transcendentals=0),
    )(parity, slot, ids, probs, tokens)


def scale_kernel(scaled_ref, cot_ref, out_ref):
    out_ref[...] = dot(scaled_ref[...], cot_ref[...]).astype(BF16)


def scale(scaled, cotangent):
    whole = pl.BlockSpec(memory_space=VMEM)
    return pl.pallas_call(
        scale_kernel,
        out_shape=jax.ShapeDtypeStruct((PADDED, QUARTER), BF16),
        in_specs=[whole] * 2,
        out_specs=whole,
        compiler_params=params(16),
        cost_estimate=pl.CostEstimate(flops=HEAVY, bytes_accessed=2_000_000, transcendentals=0),
    )(scaled, cotangent)


def combine_kernel(slot_ref, ids_ref, probs_ref, code_ref, pick_ref, back_ref, dtok_ref, dprob_ref):
    dtok_ref[...] = dot(pick_ref[...], back_ref[...], 0, 0).astype(BF16)
    chosen = jnp.where(
        iota((SLOTS, PADDED), 1) == iota((SLOTS, PADDED), 0) * BLOCK + CAP, 1.0, 0.0
    ).astype(BF16)
    scores = dot(chosen, back_ref[:, 0:TOK]) + dot(chosen, back_ref[:, TOK:2 * TOK])
    code = code_ref[...]
    placed = jnp.zeros((SLOTS, TOK), F32)
    for r in range(CAP):
        placed = placed + jnp.where(code == r + 1.0, scores[:, r:r + 1], 0.0)
    ids = ids_ref[...].astype(F32)
    probs = probs_ref[...].astype(F32)
    slot = slot_ref[...]
    found = [
        jnp.sum(jnp.where(slot == ids[k:k + 1, :], placed, 0.0), axis=0, keepdims=True)
        for k in range(4)
    ]
    dprob_ref[...] = jnp.concatenate(found, axis=0) / probs


def combine(slot, ids, probs, code, pick, back):
    whole = pl.BlockSpec(memory_space=VMEM)
    return pl.pallas_call(
        combine_kernel,
        out_shape=(
            jax.ShapeDtypeStruct((TOK, QUARTER), BF16),
            jax.ShapeDtypeStruct((4, TOK), F32),
        ),
        in_specs=[whole] * 6,
        out_specs=(whole,) * 2,
        compiler_params=params(24),
        cost_estimate=pl.CostEstimate(flops=200_000_000, bytes_accessed=2_000_000, transcendentals=0),
    )(slot, ids, probs, code, pick, back)


def half_specs(cols):
    low = pl.BlockSpec((TILE, cols), lambda m, at: (jnp.minimum(m, TILES // 2 - 1), 0))
    high = pl.BlockSpec((TILE, cols), lambda m, at: (jnp.maximum(m - TILES // 2, 0), 0))
    return [low, high]


def this_tile(refs):
    lower = pl.program_id(0) < TILES // 2
    return [jnp.where(lower, low[...], high[...]) for low, high in zip(refs[0::2], refs[1::2])]


def offset(at_ref, rel):
    return pl.multiple_of(lax.rem(at_ref[0] + rel, N_DP) * QUARTER, 128)


def weights_kernel(at_ref, wg_ref, wu_ref, wd_ref, o1, o2, o3, down, sems):
    copies = []
    for b, out in zip((1, 2, 3), (o1, o2, o3)):
        where = pl.ds(offset(at_ref, b), QUARTER)
        for i, (src, dst) in enumerate((
            (wd_ref.at[:, where], down.at[b - 1]),
            (wg_ref.at[where, :], out.at[pl.ds(0, QUARTER), :]),
            (wu_ref.at[where, :], out.at[pl.ds(QUARTER, QUARTER), :]),
        )):
            copies.append(pltpu.make_async_copy(src, dst, sems.at[b - 1, i]))
    for copy in copies:
        copy.start()
    for b, out in zip((1, 2, 3), (o1, o2, o3)):
        copies[3 * b - 3].wait()
        out[2 * QUARTER:, :] = down[b - 1].T
    for i, copy in enumerate(copies):
        if i % 3:
            copy.wait()


def weights(at, wg, wu, wd):
    whole = pl.BlockSpec(memory_space=VMEM)
    stays = pl.BlockSpec(memory_space=pl.ANY)
    return pl.pallas_call(
        weights_kernel,
        out_shape=(jax.ShapeDtypeStruct((3 * QUARTER, SHARE), BF16),) * 3,
        in_specs=[pl.BlockSpec(memory_space=pltpu.SMEM), stays, stays, stays],
        out_specs=(whole,) * 3,
        scratch_shapes=[pltpu.VMEM((3, SHARE, QUARTER), BF16), pltpu.SemaphoreType.DMA((3, 3))],
        compiler_params=params(56),
        cost_estimate=pl.CostEstimate(flops=0, bytes_accessed=9_600_000, transcendentals=0),
    )(at, wg, wu, wd)


def halves_kernel(rows_ref, a1, a2, a3, a4, low_ref, high_ref, sems):
    low = pltpu.make_async_copy(rows_ref.at[pl.ds(0, HALF), :], low_ref, sems.at[0])
    high = pltpu.make_async_copy(rows_ref.at[pl.ds(HALF, HALF), :], high_ref, sems.at[1])
    low.start()
    high.start()
    low.wait()
    high.wait()


def halves(rows, after):
    whole = pl.BlockSpec(memory_space=VMEM)
    return pl.pallas_call(
        halves_kernel,
        out_shape=(jax.ShapeDtypeStruct((HALF, QUARTER), BF16),) * 2,
        in_specs=[pl.BlockSpec(memory_space=pl.ANY)] * 5,
        out_specs=(whole,) * 2,
        scratch_shapes=[pltpu.SemaphoreType.DMA((2,))],
        compiler_params=params(56),
        cost_estimate=pl.CostEstimate(flops=HEAVY, bytes_accessed=2_800_000, transcendentals=0),
    )(rows, *after)


def near_kernel(at_ref, *refs):
    wg_ref, wu_ref, out_ref = refs[6:]
    gate = jnp.zeros((TILE, SHARE), F32)
    up = jnp.zeros((TILE, SHARE), F32)
    for rel, part in zip((0, 3, 1), this_tile(refs[:6])):
        where = pl.ds(offset(at_ref, rel), QUARTER)
        gate = gate + dot(part, wg_ref[where, :])
        up = up + dot(part, wu_ref[where, :])
    out_ref[:, :SHARE] = gate
    out_ref[:, SHARE:] = up


def near(at, parts, wg, wu):
    whole = pl.BlockSpec((WIDTH, SHARE), lambda m, at: (0, 0))
    return pl.pallas_call(
        near_kernel,
        out_shape=jax.ShapeDtypeStruct((PADDED, 2 * SHARE), F32),
        grid_spec=pltpu.PrefetchScalarGridSpec(
            num_scalar_prefetch=1, grid=(TILES,),
            in_specs=half_specs(QUARTER) * 3 + [whole, whole],
            out_specs=pl.BlockSpec((TILE, 2 * SHARE), lambda m, at: (m, 0)),
        ),
        compiler_params=params(32),
        cost_estimate=pl.CostEstimate(
            flops=3 * PADDED * WIDTH * SHARE, bytes_accessed=9_000_000, transcendentals=0
        ),
    )(at, *parts, wg, wu)


def forward_kernel(at_ref, low, high, sum_ref, wg_ref, wu_ref, hid_ref, act_ref, ups_ref):
    part = this_tile((low, high))[0]
    gate = sum_ref[:, :SHARE] + dot(part, wg_ref[...])
    up = sum_ref[:, SHARE:] + dot(part, wu_ref[...])
    sig = jax.nn.sigmoid(gate)
    act = gate * sig
    hid_ref[...] = (act * up).astype(BF16)
    act_ref[...] = act
    ups_ref[...] = up * (sig * (1.0 + gate * (1.0 - sig)))


def forward(at, far, summed, wg, wu):
    tile = pl.BlockSpec((TILE, SHARE), lambda m, at: (m, 0))
    rows = pl.BlockSpec((QUARTER, SHARE), lambda m, at: (lax.rem(at[0] + 2, N_DP), 0))
    return pl.pallas_call(
        forward_kernel,
        out_shape=(
            jax.ShapeDtypeStruct((PADDED, SHARE), BF16),
            jax.ShapeDtypeStruct((PADDED, SHARE), F32),
            jax.ShapeDtypeStruct((PADDED, SHARE), F32),
        ),
        grid_spec=pltpu.PrefetchScalarGridSpec(
            num_scalar_prefetch=1, grid=(TILES,),
            in_specs=half_specs(QUARTER)
            + [pl.BlockSpec((TILE, 2 * SHARE), lambda m, at: (m, 0)), rows, rows],
            out_specs=(tile,) * 3,
        ),
        compiler_params=params(32),
        cost_estimate=pl.CostEstimate(
            flops=PADDED * WIDTH * SHARE, bytes_accessed=4_000_000, transcendentals=PADDED * SHARE
        ),
    )(at, *far, summed, wg, wu)


def terms_kernel(at_ref, rows_ref, w0, w1, w2, w3, own_ref, p1, p2, p3):
    rows = rows_ref[...]
    own_ref[...] = dot(rows, w0[...], 1, 1)
    for w, p in ((w1, p1), (w2, p2), (w3, p3)):
        p[...] = dot(rows, w[...]).astype(BF16)


def terms(at, rows, wd, blocks):
    tile = pl.BlockSpec((TILE, SHARE), lambda m, at: (m, 0))
    down = pl.BlockSpec((QUARTER, SHARE), lambda m, at: (2, 0))
    sent = jax.ShapeDtypeStruct((PADDED, SHARE), BF16)
    return pl.pallas_call(
        terms_kernel,
        out_shape=(jax.ShapeDtypeStruct((PADDED, SHARE), F32), sent, sent, sent),
        grid_spec=pltpu.PrefetchScalarGridSpec(
            num_scalar_prefetch=1, grid=(TILES,),
            in_specs=[
                pl.BlockSpec((TILE, QUARTER), lambda m, at: (m, 0)),
                pl.BlockSpec((SHARE, QUARTER), lambda m, at: (0, at[0])),
                down, down, down,
            ],
            out_specs=(tile,) * 4,
        ),
        compiler_params=params(56),
        cost_estimate=pl.CostEstimate(
            flops=2 * PADDED * WIDTH * SHARE, bytes_accessed=5_000_000, transcendentals=0
        ),
    )(at, rows, wd, *blocks)


def within_block(shape):
    number = iota(shape, 0).astype(F32)
    return number - BLOCK * jnp.floor((number + 0.5) * (1.0 / BLOCK))


def slopes_kernel(own, r1, r2, r3, hid_ref, act_ref, ups_ref, out_ref):
    d_hidden = own[...] + r1[...].astype(F32) + r2[...].astype(F32) + r3[...].astype(F32)
    dg = d_hidden * ups_ref[...]
    du = d_hidden * act_ref[...]
    score = jnp.sum(hid_ref[...].astype(F32) * d_hidden, axis=1, keepdims=True)
    lanes = jnp.where(iota((TILE, TOK), 1).astype(F32) == within_block((TILE, TOK)), score, 0.0)
    high = lanes.astype(BF16)
    rest = (lanes - high.astype(F32)).astype(BF16)
    row = iota((TILE, TILE), 0).astype(F32)
    start = row - within_block((TILE, TILE))
    col = iota((TILE, TILE), 1).astype(F32)
    spare = within_block((TILE, SHARE)) == CAP
    group = jnp.where(col >= start, jnp.where(col < start + BLOCK, 1.0, 0.0), 0.0).astype(BF16)
    moved = jnp.concatenate([dot(group, high), dot(group, rest)], axis=1)
    out_ref[:, :SHARE] = jnp.where(spare, moved, dg).astype(BF16)
    out_ref[:, SHARE:] = du.astype(BF16)


def slopes(own, others, hid, act, ups):
    tile = pl.BlockSpec((TILE, SHARE), lambda m: (m, 0))
    return pl.pallas_call(
        slopes_kernel,
        out_shape=jax.ShapeDtypeStruct((PADDED, 2 * SHARE), BF16),
        grid=(TILES,),
        in_specs=[tile] * 7,
        out_specs=pl.BlockSpec((TILE, 2 * SHARE), lambda m: (m, 0)),
        compiler_params=params(24),
        cost_estimate=pl.CostEstimate(flops=50_000_000, bytes_accessed=5_000_000, transcendentals=0),
    )(own, *others, hid, act, ups)


def product(slope, blocks):
    return dot(slope[:, :SHARE], blocks[0], 1, 1) + dot(slope[:, SHARE:], blocks[1], 1, 1)


def back_near_kernel(at_ref, own, below, above, wg_ref, wu_ref, g1, g3, out_ref):
    total = product(own, (wg_ref[...], wu_ref[...]))
    for slope, g in ((below, g1), (above, g3)):
        total = total + product(slope, (g[:QUARTER, :], g[QUARTER:, :]))
    out_ref[...] = total


def back_kernel(at_ref, own, below, above, low, high, sum_ref, g2, out_ref):
    far = this_tile((low, high))[0]
    total = sum_ref[...] + product(far, (g2[:QUARTER, :], g2[QUARTER:, :]))
    out_ref[...] = total.astype(BF16)
    parts = [s[:, :SHARE].astype(F32) for s in (own, below, above, far)]
    lanes = (parts[0] + parts[3]) + (parts[1] + parts[2])
    score = lanes[:, :TOK] + lanes[:, TOK:]
    high = score.astype(BF16)
    rest = (score - high.astype(F32)).astype(BF16)
    spare = within_block((TILE, TOK)) == CAP
    out_ref[:, :TOK] = jnp.where(spare, high.astype(F32), total[:, :TOK]).astype(BF16)
    out_ref[:, TOK:2 * TOK] = jnp.where(spare, rest.astype(F32), total[:, TOK:2 * TOK]).astype(BF16)


def back_near(at, parts, wg, wu, blocks):
    slope = pl.BlockSpec((TILE, 2 * SHARE), lambda m, at: (m, 0))
    mine = pl.BlockSpec((QUARTER, SHARE), lambda m, at: (at[0], 0))
    both = pl.BlockSpec((2 * QUARTER, SHARE), lambda m, at: (0, 0))
    return pl.pallas_call(
        back_near_kernel,
        out_shape=jax.ShapeDtypeStruct((PADDED, QUARTER), F32),
        grid_spec=pltpu.PrefetchScalarGridSpec(
            num_scalar_prefetch=1, grid=(TILES,),
            in_specs=[slope] * 3 + [mine, mine, both, both],
            out_specs=pl.BlockSpec((TILE, QUARTER), lambda m, at: (m, 0)),
        ),
        compiler_params=params(32),
        cost_estimate=pl.CostEstimate(
            flops=3 * PADDED * WIDTH * SHARE, bytes_accessed=8_000_000, transcendentals=0
        ),
    )(at, *parts, wg, wu, blocks[0], blocks[2])


def back_rows(at, parts, summed, block):
    both = pl.BlockSpec((2 * QUARTER, SHARE), lambda m, at: (0, 0))
    slope = pl.BlockSpec((TILE, 2 * SHARE), lambda m, at: (m, 0))
    tile = pl.BlockSpec((TILE, QUARTER), lambda m, at: (m, 0))
    return pl.pallas_call(
        back_kernel,
        out_shape=jax.ShapeDtypeStruct((PADDED, QUARTER), BF16),
        grid_spec=pltpu.PrefetchScalarGridSpec(
            num_scalar_prefetch=1, grid=(TILES,),
            in_specs=[slope] * 3 + half_specs(2 * SHARE) + [tile, both], out_specs=tile,
        ),
        compiler_params=params(32),
        cost_estimate=pl.CostEstimate(
            flops=PADDED * WIDTH * SHARE, bytes_accessed=8_000_000, transcendentals=0
        ),
    )(at, *parts, summed, block)


def turn_kernel(*refs):
    half = len(refs) // 3 * 2
    for i, out in enumerate(refs[half:]):
        for c in range(QUARTER // TOK):
            cols = slice(c * TOK, (c + 1) * TOK)
            out[cols, :HALF] = refs[2 * i][:, cols].T
            out[cols, HALF:] = refs[2 * i + 1][:, cols].T


def turn(parts):
    whole = pl.BlockSpec(memory_space=VMEM)
    n = len(parts) // 2
    return pl.pallas_call(
        turn_kernel,
        out_shape=(jax.ShapeDtypeStruct((QUARTER, PADDED), BF16),) * n,
        in_specs=[whole] * (2 * n),
        out_specs=(whole,) * n,
        compiler_params=params(24),
        cost_estimate=pl.CostEstimate(flops=0, bytes_accessed=3_000_000 * n, transcendentals=0),
    )(*parts)


def grads_kernel(at_ref, x0, x1, x2, x3, slope_ref, gg_ref, gu_ref):
    slope = slope_ref[...]
    step = QUARTER // 4
    for rel, x in zip((0, 3, 1, 2), (x0, x1, x2, x3)):
        base = offset(at_ref, rel)

        def body(c, _, x=x, base=base):
            grad = dot(x[pl.ds(pl.multiple_of(c * step, 32), step), :], slope).astype(BF16)
            to = pl.ds(pl.multiple_of(base + c * step, 32), step)
            gg_ref[to, :] = grad[:, :SHARE]
            gu_ref[to, :] = grad[:, SHARE:]
            return 0

        lax.fori_loop(0, 4, body, 0)


def grads(at, xs, slope):
    whole = pl.BlockSpec(memory_space=VMEM)
    return pl.pallas_call(
        grads_kernel,
        out_shape=(jax.ShapeDtypeStruct((WIDTH, SHARE), BF16),) * 2,
        in_specs=[pl.BlockSpec(memory_space=pltpu.SMEM)] + [whole] * 5,
        out_specs=(whole,) * 2,
        compiler_params=params(32),
        cost_estimate=pl.CostEstimate(
            flops=4 * PADDED * WIDTH * SHARE, bytes_accessed=11_000_000, transcendentals=0
        ),
    )(at, *xs, slope)


def down_kernel(h0, h1, h2, h3, rows_ref, *outs):
    for h, out in zip((h0, h1, h2, h3), outs):
        out[...] = dot(h[...], rows_ref[...], 0, 0).astype(BF16)


def down_grads(hids, rows):
    whole = pl.BlockSpec(memory_space=VMEM)
    return pl.pallas_call(
        down_kernel,
        out_shape=(jax.ShapeDtypeStruct((SHARE, QUARTER), BF16),) * N_DP,
        in_specs=[whole] * 5,
        out_specs=(whole,) * N_DP,
        compiler_params=params(24),
        cost_estimate=pl.CostEstimate(
            flops=HEAVY, bytes_accessed=5_000_000, transcendentals=0
        ),
    )(*hids, rows)


def join_kernel(slot_ref, here_ref, *refs):
    n = len(refs) // 3
    same = slot_ref[here_ref[0]] == slot_ref[here_ref[0] ^ 1]
    for mine_ref, other_ref, out_ref in zip(refs[:n], refs[n:2 * n], refs[2 * n:]):
        mine = mine_ref[...].astype(F32)
        out_ref[...] = jnp.where(same, mine + other_ref[...].astype(F32), mine).astype(BF16)


def join(slot_expert, here, mine, steps):
    other = [swap(array) for array in mine]
    rows, cols = mine[0].shape
    block = pl.BlockSpec((rows // steps, cols), lambda m, slot, here: (m, 0))
    return pl.pallas_call(
        join_kernel,
        out_shape=(jax.ShapeDtypeStruct((rows, cols), BF16),) * len(mine),
        grid_spec=pltpu.PrefetchScalarGridSpec(
            num_scalar_prefetch=2, grid=(steps,),
            in_specs=[block] * (2 * len(mine)), out_specs=(block,) * len(mine),
        ),
        compiler_params=params(24),
        cost_estimate=pl.CostEstimate(flops=0, bytes_accessed=0, transcendentals=0),
    )(slot_expert, here, *mine, *other)


def place_kernel(at_ref, p0, p1, p2, p3, out_ref):
    for rel, p in enumerate((p0, p1, p2, p3)):
        out_ref[:, pl.ds(offset(at_ref, rel), QUARTER)] = p[...]


def placed(at, parts):
    whole = pl.BlockSpec(memory_space=VMEM)
    return pl.pallas_call(
        place_kernel,
        out_shape=jax.ShapeDtypeStruct((SHARE, WIDTH), BF16),
        in_specs=[pl.BlockSpec(memory_space=pltpu.SMEM)] + [whole] * 4,
        out_specs=whole,
        compiler_params=params(16),
        cost_estimate=pl.CostEstimate(flops=0, bytes_accessed=0, transcendentals=0),
    )(at, *parts)


def shift(x, by):
    return lax.ppermute(x, "dp", [(i, (i + by) % N_DP) for i in range(N_DP)])


def swap(x):
    return lax.ppermute(x, "expert", [(i, i ^ 1) for i in range(SLOTS)])


def exchange(rows):
    return lax.all_to_all(
        rows.reshape(SLOTS, 3, 4, QUARTER), "expert", split_axis=0, concat_axis=0, tiled=True
    )


def ring(low, high):
    low_below, high_above = shift(low, 1), shift(high, -1)
    high_below, low_above = shift(high, 1), shift(low, -1)
    far = [shift(low_below, 1), shift(high_above, -1)]
    return [low, high], [low_below, high_below], [low_above, high_above], far


def ordered(arrays):
    return lax.optimization_barrier(arrays)


def shards(tokens, cotangent, expert_ids, gate_probs, slot_expert, w_gate, w_up, w_down):
    here = lax.axis_index("expert")
    at = lax.axis_index("dp").reshape(1)
    parity = (here % 2).reshape(1)
    wg, wu, wd = w_gate[0], w_up[0], w_down[0]
    ids, probs = expert_ids.T, gate_probs.T
    slot = jnp.broadcast_to(slot_expert.astype(F32)[:, None], (SLOTS, TOK))
    x_rows, code, pick, scaled = pack(parity, slot, ids, probs, tokens)
    d_rows = scale(scaled, cotangent)
    sent = weights(at, wg, wu, wd)
    blocks = [shift(w, b) for w, b in zip(sent, (1, 2, 3))]
    x_rows, token = ordered((x_rows, swap(sent[0][:16])))
    x_here = exchange(x_rows).reshape(PADDED, QUARTER)
    x_own, x_below, x_above, x_far = ring(*halves(x_here, (*blocks, token)))
    d_here = exchange(d_rows).reshape(PADDED, QUARTER)

    own, *out = terms(at, d_here, wd, blocks)
    others = [shift(out[b - 1], -b) for b in (2, 1, 3)]
    x_parts, own = ordered((x_own + x_below + x_above, own))
    hid, act, ups = forward(at, x_far, near(at, x_parts, wg, wu), wg, wu)
    slope = slopes(own, others, hid, act, ups)
    s_below, s_above = shift(slope, 1), shift(slope, -1)
    x_turned = turn(ordered((x_parts + x_far, slope))[0])
    s_below, s_above, x_turned = ordered((s_below, s_above, x_turned))
    s_far = [shift(s_below[:HALF], 1), shift(s_above[HALF:], -1)]
    s_near = (slope, s_below, s_above)
    s_far, summed = ordered((s_far, back_near(at, s_near, wg, wu, blocks)))
    pay = back_rows(at, (*s_near, *s_far), summed, blocks[1])
    back = exchange(pay).reshape(PADDED, QUARTER)
    d_tokens, d_probs = combine(slot, ids, probs, code, pick, back)

    hid = ordered((hid, s_far))[0]
    pieces = down_grads([hid] + [shift(hid, b) for b in (1, 2, 3)], d_here)
    down = placed(at, [pieces[0]] + [shift(pieces[b], -b) for b in (1, 2, 3)])
    grad_gate, grad_up = join(slot_expert, here.reshape(1), grads(at, x_turned, ordered((slope, pay))[0]), 4)
    grad_down = join(slot_expert, here.reshape(1), [down], 2)[0]
    return d_tokens, d_probs.T, grad_gate[None], grad_up[None], grad_down[None]


def solution(mesh):
    specs = (
        P("expert", "dp"),
        P("expert", "dp"),
        P("expert", None),
        P("expert", None),
        P(),
        P("expert", None, "dp"),
        P("expert", None, "dp"),
        P("expert", "dp", None),
    )
    return jax.shard_map(
        shards,
        mesh=mesh,
        in_specs=specs,
        out_specs=(
            P("expert", "dp"),
            P("expert", None),
            P("expert", None, "dp"),
            P("expert", None, "dp"),
            P("expert", "dp", None),
        ),
        check_vma=False,
    )
```

```python
import functools

import jax
import jax.numpy as jnp
from jax import lax
from jax.experimental import pallas as pl
from jax.experimental.pallas import tpu as pltpu
from jax.sharding import PartitionSpec as P

F32 = jnp.float32
BF16 = jnp.bfloat16
SLOTS = 64
CAP = 11
BLOCK = 12
TOK = 128
PADDED = SLOTS * BLOCK
FOURS = PADDED // 4
HALF = PADDED // 2
QUARTER = 896
WIDTH = 3584
SHARE = 256
N_DP = 4
TILE = 192
TILES = PADDED // TILE
VMEM = pltpu.VMEM
HEAVY = 40_000_000_000


def iota(shape, dim):
    return lax.broadcasted_iota(jnp.int32, shape, dim)


def dot(left, right, left_dim=1, right_dim=0, precision=None):
    return lax.dot_general(
        left, right, (((left_dim,), (right_dim,)), ((), ())),
        precision=precision, preferred_element_type=F32,
    )


def params(mib):
    return pltpu.CompilerParams(vmem_limit_bytes=mib << 20)


def pack_kernel(parity_ref, slot_ref, ids_ref, probs_ref, tok_ref, x_ref, code_ref, pick_ref, scaled_ref):
    slot = slot_ref[...]
    index = iota((SLOTS, TOK), 0)
    second = (index & 1).astype(F32)
    partner = jnp.where(second > 0, pltpu.roll(slot, 1, 0), pltpu.roll(slot, SLOTS - 1, 0))
    paired = slot == partner
    ids = ids_ref[...].astype(F32)
    probs = probs_ref[...].astype(F32)
    chosen = jnp.zeros((SLOTS, TOK), F32)
    weight = jnp.zeros((SLOTS, TOK), F32)
    for k in range(4):
        here = slot == ids[k:k + 1, :]
        chosen = chosen + jnp.where(here, 1.0, 0.0)
        weight = weight + jnp.where(here, probs[k:k + 1, :], 0.0)
    earlier = jnp.where(iota((TOK, TOK), 0) < iota((TOK, TOK), 1), 1.0, 0.0).astype(BF16)
    rank = dot(chosen.astype(BF16), earlier)
    shifted = rank + parity_ref[0].astype(F32)
    half = jnp.floor(shifted * 0.5)
    taken = jnp.where(paired, jnp.where(shifted - 2.0 * half == second, 1.0, 0.0), 1.0) * chosen
    place = jnp.where(paired, half, rank)
    code = jnp.where(taken > 0, place + 1.0, 0.0)
    code_ref[...] = code
    row, col = iota((PADDED, SLOTS), 0), iota((PADDED, SLOTS), 1) * BLOCK
    spread = jnp.where(row >= col, jnp.where(row < col + BLOCK, 1.0, 0.0), 0.0).astype(BF16)
    number = iota((PADDED, TOK), 0).astype(F32)
    within = number - BLOCK * jnp.floor((number + 0.5) * (1.0 / BLOCK)) + 1.0
    pick = jnp.where(dot(spread, code.astype(BF16)) == within, 1.0, 0.0)
    scaled = pick * dot(spread, weight.astype(BF16))
    pick = pick.astype(BF16)
    pick_ref[...] = pick
    scaled_ref[...] = scaled.astype(BF16)
    x_ref[...] = dot(pick, tok_ref[...]).astype(BF16).reshape(FOURS, 4, QUARTER)


def pack(parity, slot, ids, probs, tokens):
    whole = pl.BlockSpec(memory_space=VMEM)
    return pl.pallas_call(
        pack_kernel,
        out_shape=(
            jax.ShapeDtypeStruct((FOURS, 4, QUARTER), BF16),
            jax.ShapeDtypeStruct((SLOTS, TOK), F32),
            jax.ShapeDtypeStruct((PADDED, TOK), BF16),
            jax.ShapeDtypeStruct((PADDED, TOK), BF16),
        ),
        in_specs=[pl.BlockSpec(memory_space=pltpu.SMEM)] + [whole] * 4,
        out_specs=(whole,) * 4,
        compiler_params=params(56),
        cost_estimate=pl.CostEstimate(flops=HEAVY, bytes_accessed=3_000_000, transcendentals=0),
    )(parity, slot, ids, probs, tokens)


def scale_kernel(scaled_ref, cot_ref, out_ref):
    out_ref[...] = dot(scaled_ref[...], cot_ref[...]).astype(BF16).reshape(FOURS, 4, QUARTER)


def scale(scaled, cotangent):
    whole = pl.BlockSpec(memory_space=VMEM)
    return pl.pallas_call(
        scale_kernel,
        out_shape=jax.ShapeDtypeStruct((FOURS, 4, QUARTER), BF16),
        in_specs=[whole] * 2,
        out_specs=whole,
        compiler_params=params(16),
        cost_estimate=pl.CostEstimate(flops=HEAVY, bytes_accessed=2_000_000, transcendentals=0),
    )(scaled, cotangent)


def combine_kernel(slot_ref, ids_ref, probs_ref, code_ref, pick_ref, back_ref, dtok_ref, dprob_ref):
    back = back_ref[...].reshape(PADDED, QUARTER)
    dtok_ref[...] = dot(pick_ref[...], back, 0, 0).astype(BF16)
    chosen = jnp.where(
        iota((SLOTS, PADDED), 1) == iota((SLOTS, PADDED), 0) * BLOCK + CAP, 1.0, 0.0
    ).astype(BF16)
    scores = dot(chosen, back[:, 0:TOK]) + dot(chosen, back[:, TOK:2 * TOK])
    code = code_ref[...]
    placed = jnp.zeros((SLOTS, TOK), F32)
    for r in range(CAP):
        placed = placed + jnp.where(code == r + 1.0, scores[:, r:r + 1], 0.0)
    ids = ids_ref[...].astype(F32)
    probs = probs_ref[...].astype(F32)
    slot = slot_ref[...]
    found = [
        jnp.sum(jnp.where(slot == ids[k:k + 1, :], placed, 0.0), axis=0, keepdims=True)
        for k in range(4)
    ]
    dprob_ref[...] = jnp.concatenate(found, axis=0) / probs


def combine(slot, ids, probs, code, pick, back):
    whole = pl.BlockSpec(memory_space=VMEM)
    return pl.pallas_call(
        combine_kernel,
        out_shape=(
            jax.ShapeDtypeStruct((TOK, QUARTER), BF16),
            jax.ShapeDtypeStruct((4, TOK), F32),
        ),
        in_specs=[whole] * 6,
        out_specs=(whole,) * 2,
        compiler_params=params(24),
        cost_estimate=pl.CostEstimate(flops=200_000_000, bytes_accessed=2_000_000, transcendentals=0),
    )(slot, ids, probs, code, pick, back)


def half_specs(cols):
    low = pl.BlockSpec((TILE, cols), lambda m, at: (jnp.minimum(m, TILES // 2 - 1), 0))
    high = pl.BlockSpec((TILE, cols), lambda m, at: (jnp.maximum(m - TILES // 2, 0), 0))
    return [low, high]


def this_tile(refs):
    lower = pl.program_id(0) < TILES // 2
    return [jnp.where(lower, low[...], high[...]) for low, high in zip(refs[0::2], refs[1::2])]


def offset(at_ref, rel):
    return pl.multiple_of(lax.rem(at_ref[0] + rel, N_DP) * QUARTER, 128)


def weights_kernel(at_ref, wg_ref, wu_ref, wd_ref, o1, o2, o3, token, down, sems):
    copies = []
    for b, out in zip((1, 2, 3), (o1, o2, o3)):
        where = pl.ds(offset(at_ref, b), QUARTER)
        for i, (src, dst) in enumerate((
            (wd_ref.at[:, where], down.at[b - 1]),
            (wg_ref.at[where, :], out.at[pl.ds(0, QUARTER), :]),
            (wu_ref.at[where, :], out.at[pl.ds(QUARTER, QUARTER), :]),
        )):
            copies.append(pltpu.make_async_copy(src, dst, sems.at[b - 1, i]))
    for copy in copies:
        copy.start()
    for b, out in zip((1, 2, 3), (o1, o2, o3)):
        copies[3 * b - 3].wait()
        out[2 * QUARTER:, :] = down[b - 1].T
    token[...] = down[0, :16, :TOK]
    for i, copy in enumerate(copies):
        if i % 3:
            copy.wait()


def weights(at, wg, wu, wd):
    whole = pl.BlockSpec(memory_space=VMEM)
    stays = pl.BlockSpec(memory_space=pl.ANY)
    return pl.pallas_call(
        weights_kernel,
        out_shape=(jax.ShapeDtypeStruct((3 * QUARTER, SHARE), BF16),) * 3
        + (jax.ShapeDtypeStruct((16, TOK), BF16),),
        in_specs=[pl.BlockSpec(memory_space=pltpu.SMEM), stays, stays, stays],
        out_specs=(whole,) * 4,
        scratch_shapes=[pltpu.VMEM((3, SHARE, QUARTER), BF16), pltpu.SemaphoreType.DMA((3, 3))],
        compiler_params=params(56),
        cost_estimate=pl.CostEstimate(flops=0, bytes_accessed=9_600_000, transcendentals=0),
    )(at, wg, wu, wd)


def halves_kernel(rows_ref, after_ref, low_ref, high_ref):
    rows = rows_ref[...].reshape(HALF, QUARTER)

    @pl.when(pl.program_id(0) == 0)
    def _():
        low_ref[...] = rows

    @pl.when(pl.program_id(0) == 1)
    def _():
        high_ref[...] = rows


def halves(rows, after):
    half = pl.BlockSpec((HALF, QUARTER), lambda m: (0, 0))
    return pl.pallas_call(
        halves_kernel,
        out_shape=(jax.ShapeDtypeStruct((HALF, QUARTER), BF16),) * 2,
        grid=(2,),
        in_specs=[
            pl.BlockSpec((FOURS // 2, 4, QUARTER), lambda m: (m, 0, 0)),
            pl.BlockSpec(memory_space=pl.ANY),
        ],
        out_specs=(half,) * 2,
        compiler_params=params(56),
        cost_estimate=pl.CostEstimate(flops=HEAVY, bytes_accessed=2_800_000, transcendentals=0),
    )(rows, after)


def near_kernel(at_ref, *refs):
    wg_ref, wu_ref, out_ref = refs[6:]
    gate = jnp.zeros((TILE, SHARE), F32)
    up = jnp.zeros((TILE, SHARE), F32)
    for rel, part in zip((0, 3, 1), this_tile(refs[:6])):
        where = pl.ds(offset(at_ref, rel), QUARTER)
        gate = gate + dot(part, wg_ref[where, :])
        up = up + dot(part, wu_ref[where, :])
    out_ref[:, :SHARE] = gate
    out_ref[:, SHARE:] = up


def near(at, parts, wg, wu):
    whole = pl.BlockSpec((WIDTH, SHARE), lambda m, at: (0, 0))
    return pl.pallas_call(
        near_kernel,
        out_shape=jax.ShapeDtypeStruct((PADDED, 2 * SHARE), F32),
        grid_spec=pltpu.PrefetchScalarGridSpec(
            num_scalar_prefetch=1, grid=(TILES,),
            in_specs=half_specs(QUARTER) * 3 + [whole, whole],
            out_specs=pl.BlockSpec((TILE, 2 * SHARE), lambda m, at: (m, 0)),
        ),
        compiler_params=params(32),
        cost_estimate=pl.CostEstimate(
            flops=3 * PADDED * WIDTH * SHARE, bytes_accessed=9_000_000, transcendentals=0
        ),
    )(at, *parts, wg, wu)


def forward_kernel(at_ref, low, high, sum_ref, wg_ref, wu_ref, hid_ref, act_ref, ups_ref):
    part = this_tile((low, high))[0]
    gate = sum_ref[:, :SHARE] + dot(part, wg_ref[...])
    up = sum_ref[:, SHARE:] + dot(part, wu_ref[...])
    sig = jax.nn.sigmoid(gate)
    act = gate * sig
    hid_ref[...] = (act * up).astype(BF16)
    act_ref[...] = act
    ups_ref[...] = up * (sig * (1.0 + gate * (1.0 - sig)))


def forward(at, far, summed, wg, wu):
    tile = pl.BlockSpec((TILE, SHARE), lambda m, at: (m, 0))
    rows = pl.BlockSpec((QUARTER, SHARE), lambda m, at: (lax.rem(at[0] + 2, N_DP), 0))
    return pl.pallas_call(
        forward_kernel,
        out_shape=(
            jax.ShapeDtypeStruct((PADDED, SHARE), BF16),
            jax.ShapeDtypeStruct((PADDED, SHARE), F32),
            jax.ShapeDtypeStruct((PADDED, SHARE), F32),
        ),
        grid_spec=pltpu.PrefetchScalarGridSpec(
            num_scalar_prefetch=1, grid=(TILES,),
            in_specs=half_specs(QUARTER)
            + [pl.BlockSpec((TILE, 2 * SHARE), lambda m, at: (m, 0)), rows, rows],
            out_specs=(tile,) * 3,
        ),
        compiler_params=params(32),
        cost_estimate=pl.CostEstimate(
            flops=PADDED * WIDTH * SHARE, bytes_accessed=4_000_000, transcendentals=PADDED * SHARE
        ),
    )(at, *far, summed, wg, wu)


def terms_kernel(at_ref, rows_ref, w0, w1, w2, w3, own_ref, p1, p2, p3):
    rows = rows_ref[...].reshape(TILE, QUARTER)
    own_ref[...] = dot(rows, w0[...], 1, 1)
    for w, p in ((w1, p1), (w2, p2), (w3, p3)):
        p[...] = dot(rows, w[...]).astype(BF16)


def terms(at, rows, wd, blocks):
    tile = pl.BlockSpec((TILE, SHARE), lambda m, at: (m, 0))
    down = pl.BlockSpec((QUARTER, SHARE), lambda m, at: (2, 0))
    sent = jax.ShapeDtypeStruct((PADDED, SHARE), BF16)
    return pl.pallas_call(
        terms_kernel,
        out_shape=(jax.ShapeDtypeStruct((PADDED, SHARE), F32), sent, sent, sent),
        grid_spec=pltpu.PrefetchScalarGridSpec(
            num_scalar_prefetch=1, grid=(TILES,),
            in_specs=[
                pl.BlockSpec((TILE // 4, 4, QUARTER), lambda m, at: (m, 0, 0)),
                pl.BlockSpec((SHARE, QUARTER), lambda m, at: (0, at[0])),
                down, down, down,
            ],
            out_specs=(tile,) * 4,
        ),
        compiler_params=params(56),
        cost_estimate=pl.CostEstimate(
            flops=2 * PADDED * WIDTH * SHARE, bytes_accessed=5_000_000, transcendentals=0
        ),
    )(at, rows, wd, *blocks)


def within_block(shape):
    number = iota(shape, 0).astype(F32)
    return number - BLOCK * jnp.floor((number + 0.5) * (1.0 / BLOCK))


def slopes_kernel(own, r1, r2, r3, hid_ref, act_ref, ups_ref, out_ref):
    d_hidden = own[...] + r1[...].astype(F32) + r2[...].astype(F32) + r3[...].astype(F32)
    dg = d_hidden * ups_ref[...]
    du = d_hidden * act_ref[...]
    score = jnp.sum(hid_ref[...].astype(F32) * d_hidden, axis=1, keepdims=True)
    lanes = jnp.where(iota((TILE, TOK), 1).astype(F32) == within_block((TILE, TOK)), score, 0.0)
    high = lanes.astype(BF16)
    rest = (lanes - high.astype(F32)).astype(BF16)
    row = iota((TILE, TILE), 0).astype(F32)
    start = row - within_block((TILE, TILE))
    col = iota((TILE, TILE), 1).astype(F32)
    spare = within_block((TILE, SHARE)) == CAP
    group = jnp.where(col >= start, jnp.where(col < start + BLOCK, 1.0, 0.0), 0.0).astype(BF16)
    moved = jnp.concatenate([dot(group, high), dot(group, rest)], axis=1)
    out_ref[:, :SHARE] = jnp.where(spare, moved, dg).astype(BF16)
    out_ref[:, SHARE:] = du.astype(BF16)


def slopes(own, others, hid, act, ups):
    tile = pl.BlockSpec((TILE, SHARE), lambda m: (m, 0))
    return pl.pallas_call(
        slopes_kernel,
        out_shape=jax.ShapeDtypeStruct((PADDED, 2 * SHARE), BF16),
        grid=(TILES,),
        in_specs=[tile] * 7,
        out_specs=pl.BlockSpec((TILE, 2 * SHARE), lambda m: (m, 0)),
        compiler_params=params(24),
        cost_estimate=pl.CostEstimate(flops=50_000_000, bytes_accessed=5_000_000, transcendentals=0),
    )(own, *others, hid, act, ups)


def product(slope, blocks):
    return dot(slope[:, :SHARE], blocks[0], 1, 1) + dot(slope[:, SHARE:], blocks[1], 1, 1)


def back_near_kernel(at_ref, own, below, above, wg_ref, wu_ref, g1, g3, out_ref):
    total = product(own, (wg_ref[...], wu_ref[...]))
    for slope, g in ((below, g1), (above, g3)):
        total = total + product(slope, (g[:QUARTER, :], g[QUARTER:, :]))
    out_ref[...] = total


def back_kernel(at_ref, own, below, above, low, high, sum_ref, g2, out_ref):
    far = this_tile((low, high))[0]
    total = sum_ref[...] + product(far, (g2[:QUARTER, :], g2[QUARTER:, :]))
    parts = [s[:, :SHARE].astype(F32) for s in (own, below, above, far)]
    lanes = (parts[0] + parts[3]) + (parts[1] + parts[2])
    score = lanes[:, :TOK] + lanes[:, TOK:]
    high = score.astype(BF16).astype(F32)
    scores = jnp.concatenate([high, score - high], axis=1)
    spare = within_block((TILE, 2 * TOK)) == CAP
    first = jnp.where(spare, scores, total[:, :2 * TOK])
    rows = jnp.concatenate([first, total[:, 2 * TOK:]], axis=1).astype(BF16)
    out_ref[...] = rows.reshape(TILE // 4, 4, QUARTER)


def back_near(at, parts, wg, wu, blocks):
    slope = pl.BlockSpec((TILE, 2 * SHARE), lambda m, at: (m, 0))
    mine = pl.BlockSpec((QUARTER, SHARE), lambda m, at: (at[0], 0))
    both = pl.BlockSpec((2 * QUARTER, SHARE), lambda m, at: (0, 0))
    return pl.pallas_call(
        back_near_kernel,
        out_shape=jax.ShapeDtypeStruct((PADDED, QUARTER), F32),
        grid_spec=pltpu.PrefetchScalarGridSpec(
            num_scalar_prefetch=1, grid=(TILES,),
            in_specs=[slope] * 3 + [mine, mine, both, both],
            out_specs=pl.BlockSpec((TILE, QUARTER), lambda m, at: (m, 0)),
        ),
        compiler_params=params(32),
        cost_estimate=pl.CostEstimate(
            flops=3 * PADDED * WIDTH * SHARE, bytes_accessed=8_000_000, transcendentals=0
        ),
    )(at, *parts, wg, wu, blocks[0], blocks[2])


def back_rows(at, parts, summed, block):
    both = pl.BlockSpec((2 * QUARTER, SHARE), lambda m, at: (0, 0))
    slope = pl.BlockSpec((TILE, 2 * SHARE), lambda m, at: (m, 0))
    tile = pl.BlockSpec((TILE, QUARTER), lambda m, at: (m, 0))
    return pl.pallas_call(
        back_kernel,
        out_shape=jax.ShapeDtypeStruct((FOURS, 4, QUARTER), BF16),
        grid_spec=pltpu.PrefetchScalarGridSpec(
            num_scalar_prefetch=1, grid=(TILES,),
            in_specs=[slope] * 3 + half_specs(2 * SHARE) + [tile, both],
            out_specs=pl.BlockSpec((TILE // 4, 4, QUARTER), lambda m, at: (m, 0, 0)),
        ),
        compiler_params=params(32),
        cost_estimate=pl.CostEstimate(
            flops=PADDED * WIDTH * SHARE, bytes_accessed=8_000_000, transcendentals=0
        ),
    )(at, *parts, summed, block)


def turn_kernel(*refs):
    half = len(refs) // 3 * 2
    for i, out in enumerate(refs[half:]):
        for c in range(QUARTER // TOK):
            cols = slice(c * TOK, (c + 1) * TOK)
            out[cols, :HALF] = refs[2 * i][:, cols].T
            out[cols, HALF:] = refs[2 * i + 1][:, cols].T


def turn(parts):
    whole = pl.BlockSpec(memory_space=VMEM)
    n = len(parts) // 2
    return pl.pallas_call(
        turn_kernel,
        out_shape=(jax.ShapeDtypeStruct((QUARTER, PADDED), BF16),) * n,
        in_specs=[whole] * (2 * n),
        out_specs=(whole,) * n,
        compiler_params=params(24),
        cost_estimate=pl.CostEstimate(flops=0, bytes_accessed=3_000_000 * n, transcendentals=0),
    )(*parts)


def grads_kernel(at_ref, x0, x1, x2, x3, slope_ref, gg_ref, gu_ref):
    slope = slope_ref[...]
    step = QUARTER // 4
    for rel, x in zip((0, 3, 1, 2), (x0, x1, x2, x3)):
        base = offset(at_ref, rel)

        def body(c, _, x=x, base=base):
            grad = dot(x[pl.ds(pl.multiple_of(c * step, 32), step), :], slope).astype(BF16)
            to = pl.ds(pl.multiple_of(base + c * step, 32), step)
            gg_ref[to, :] = grad[:, :SHARE]
            gu_ref[to, :] = grad[:, SHARE:]
            return 0

        lax.fori_loop(0, 4, body, 0)


def grads(at, xs, slope):
    whole = pl.BlockSpec(memory_space=VMEM)
    return pl.pallas_call(
        grads_kernel,
        out_shape=(jax.ShapeDtypeStruct((WIDTH, SHARE), BF16),) * 2,
        in_specs=[pl.BlockSpec(memory_space=pltpu.SMEM)] + [whole] * 5,
        out_specs=(whole,) * 2,
        compiler_params=params(32),
        cost_estimate=pl.CostEstimate(
            flops=4 * PADDED * WIDTH * SHARE, bytes_accessed=11_000_000, transcendentals=0
        ),
    )(at, *xs, slope)


def down_kernel(h0, h1, h2, h3, rows_ref, *outs):
    rows = rows_ref[...].reshape(PADDED, QUARTER)
    for h, out in zip((h0, h1, h2, h3), outs):
        out[...] = dot(h[...], rows, 0, 0).astype(BF16)


def down_grads(hids, rows):
    whole = pl.BlockSpec(memory_space=VMEM)
    return pl.pallas_call(
        down_kernel,
        out_shape=(jax.ShapeDtypeStruct((SHARE, QUARTER), BF16),) * N_DP,
        in_specs=[whole] * 5,
        out_specs=(whole,) * N_DP,
        compiler_params=params(24),
        cost_estimate=pl.CostEstimate(
            flops=HEAVY, bytes_accessed=5_000_000, transcendentals=0
        ),
    )(*hids, rows)


def join_kernel(slot_ref, here_ref, *refs):
    n = len(refs) // 3
    same = slot_ref[here_ref[0]] == slot_ref[here_ref[0] ^ 1]
    for mine_ref, other_ref, out_ref in zip(refs[:n], refs[n:2 * n], refs[2 * n:]):
        mine = mine_ref[...].astype(F32)
        out_ref[...] = jnp.where(same, mine + other_ref[...].astype(F32), mine).astype(BF16)


def join(slot_expert, here, mine, steps):
    other = [swap(array) for array in mine]
    rows, cols = mine[0].shape
    block = pl.BlockSpec((rows // steps, cols), lambda m, slot, here: (m, 0))
    return pl.pallas_call(
        join_kernel,
        out_shape=(jax.ShapeDtypeStruct((rows, cols), BF16),) * len(mine),
        grid_spec=pltpu.PrefetchScalarGridSpec(
            num_scalar_prefetch=2, grid=(steps,),
            in_specs=[block] * (2 * len(mine)), out_specs=(block,) * len(mine),
        ),
        compiler_params=params(24),
        cost_estimate=pl.CostEstimate(flops=0, bytes_accessed=0, transcendentals=0),
    )(slot_expert, here, *mine, *other)


def place_kernel(at_ref, p0, p1, p2, p3, out_ref):
    for rel, p in enumerate((p0, p1, p2, p3)):
        out_ref[:, pl.ds(offset(at_ref, rel), QUARTER)] = p[...]


def placed(at, parts):
    whole = pl.BlockSpec(memory_space=VMEM)
    return pl.pallas_call(
        place_kernel,
        out_shape=jax.ShapeDtypeStruct((SHARE, WIDTH), BF16),
        in_specs=[pl.BlockSpec(memory_space=pltpu.SMEM)] + [whole] * 4,
        out_specs=whole,
        compiler_params=params(16),
        cost_estimate=pl.CostEstimate(flops=0, bytes_accessed=0, transcendentals=0),
    )(at, *parts)


def shift(x, by):
    return lax.ppermute(x, "dp", [(i, (i + by) % N_DP) for i in range(N_DP)])


def swap(x):
    return lax.ppermute(x, "expert", [(i, i ^ 1) for i in range(SLOTS)])


def exchange(rows):
    return lax.all_to_all(
        rows.reshape(SLOTS, 3, 4, QUARTER), "expert", split_axis=0, concat_axis=0, tiled=True
    ).reshape(FOURS, 4, QUARTER)


def ring(low, high):
    low_below, high_above = shift(low, 1), shift(high, -1)
    high_below, low_above = shift(high, 1), shift(low, -1)
    far = [shift(low_below, 1), shift(high_above, -1)]
    return [low, high], [low_below, high_below], [low_above, high_above], far


def ordered(arrays):
    return lax.optimization_barrier(arrays)


def shards(tokens, cotangent, expert_ids, gate_probs, slot_expert, w_gate, w_up, w_down):
    here = lax.axis_index("expert")
    at = lax.axis_index("dp").reshape(1)
    parity = (here % 2).reshape(1)
    wg, wu, wd = w_gate[0], w_up[0], w_down[0]
    ids, probs = expert_ids.T, gate_probs.T
    slot = jnp.broadcast_to(slot_expert.astype(F32)[:, None], (SLOTS, TOK))
    x_rows, code, pick, scaled = pack(parity, slot, ids, probs, tokens)
    d_rows = scale(scaled, cotangent)
    *sent, few = weights(at, wg, wu, wd)
    blocks = [shift(w, b) for w, b in zip(sent, (1, 2, 3))]
    x_rows, token = ordered((x_rows, swap(few)))
    x_here = exchange(x_rows)
    x_own, x_below, x_above, x_far = ring(*halves(x_here, token))
    d_here = exchange(d_rows)

    own, *out = terms(at, d_here, wd, blocks)
    others = [shift(out[b - 1], -b) for b in (2, 1, 3)]
    x_parts, own = ordered((x_own + x_below + x_above, own))
    hid, act, ups = forward(at, x_far, near(at, x_parts, wg, wu), wg, wu)
    slope = slopes(own, others, hid, act, ups)
    s_below, s_above = shift(slope, 1), shift(slope, -1)
    x_turned = turn(ordered((x_parts + x_far, slope))[0])
    s_below, s_above, x_turned = ordered((s_below, s_above, x_turned))
    s_far = [shift(s_below[:HALF], 1), shift(s_above[HALF:], -1)]
    s_near = (slope, s_below, s_above)
    s_far, summed = ordered((s_far, back_near(at, s_near, wg, wu, blocks)))
    pay = back_rows(at, (*s_near, *s_far), summed, blocks[1])
    back = exchange(pay)
    d_tokens, d_probs = combine(slot, ids, probs, code, pick, back)

    hid = ordered((hid, s_far))[0]
    pieces = down_grads([hid] + [shift(hid, b) for b in (1, 2, 3)], d_here)
    down = placed(at, [pieces[0]] + [shift(pieces[b], -b) for b in (1, 2, 3)])
    grad_gate, grad_up = join(slot_expert, here.reshape(1), grads(at, x_turned, ordered((slope, pay))[0]), 4)
    grad_down = join(slot_expert, here.reshape(1), [down], 2)[0]
    return d_tokens, d_probs.T, grad_gate[None], grad_up[None], grad_down[None]


def solution(mesh):
    specs = (
        P("expert", "dp"),
        P("expert", "dp"),
        P("expert", None),
        P("expert", None),
        P(),
        P("expert", None, "dp"),
        P("expert", None, "dp"),
        P("expert", "dp", None),
    )
    return jax.shard_map(
        shards,
        mesh=mesh,
        in_specs=specs,
        out_specs=(
            P("expert", "dp"),
            P("expert", None),
            P("expert", None, "dp"),
            P("expert", None, "dp"),
            P("expert", "dp", None),
        ),
        check_vma=False,
    )
```

```python
import functools

import jax
import jax.numpy as jnp
from jax import lax
from jax.experimental import pallas as pl
from jax.experimental.pallas import tpu as pltpu
from jax.sharding import PartitionSpec as P

F32 = jnp.float32
BF16 = jnp.bfloat16
SLOTS = 64
CAP = 11
BLOCK = 12
TOK = 128
PADDED = SLOTS * BLOCK
FOURS = PADDED // 4
HALF = PADDED // 2
QUARTER = 896
WIDTH = 3584
SHARE = 256
N_DP = 4
TILE = 192
TILES = PADDED // TILE
VMEM = pltpu.VMEM
HEAVY = 40_000_000_000


def iota(shape, dim):
    return lax.broadcasted_iota(jnp.int32, shape, dim)


def dot(left, right, left_dim=1, right_dim=0, precision=None):
    return lax.dot_general(
        left, right, (((left_dim,), (right_dim,)), ((), ())),
        precision=precision, preferred_element_type=F32,
    )


def params(mib):
    return pltpu.CompilerParams(vmem_limit_bytes=mib << 20)


def pack_kernel(parity_ref, slot_ref, ids_ref, probs_ref, tok_ref, x_ref, code_ref, pick_ref, scaled_ref):
    slot = slot_ref[...]
    index = iota((SLOTS, TOK), 0)
    second = (index & 1).astype(F32)
    partner = jnp.where(second > 0, pltpu.roll(slot, 1, 0), pltpu.roll(slot, SLOTS - 1, 0))
    paired = slot == partner
    ids = ids_ref[...].astype(F32)
    probs = probs_ref[...].astype(F32)
    chosen = jnp.zeros((SLOTS, TOK), F32)
    weight = jnp.zeros((SLOTS, TOK), F32)
    for k in range(4):
        here = slot == ids[k:k + 1, :]
        chosen = chosen + jnp.where(here, 1.0, 0.0)
        weight = weight + jnp.where(here, probs[k:k + 1, :], 0.0)
    earlier = jnp.where(iota((TOK, TOK), 0) < iota((TOK, TOK), 1), 1.0, 0.0).astype(BF16)
    rank = dot(chosen.astype(BF16), earlier)
    shifted = rank + parity_ref[0].astype(F32)
    half = jnp.floor(shifted * 0.5)
    taken = jnp.where(paired, jnp.where(shifted - 2.0 * half == second, 1.0, 0.0), 1.0) * chosen
    place = jnp.where(paired, half, rank)
    code = jnp.where(taken > 0, place + 1.0, 0.0)
    code_ref[...] = code
    row, col = iota((PADDED, SLOTS), 0), iota((PADDED, SLOTS), 1) * BLOCK
    spread = jnp.where(row >= col, jnp.where(row < col + BLOCK, 1.0, 0.0), 0.0).astype(BF16)
    number = iota((PADDED, TOK), 0).astype(F32)
    within = number - BLOCK * jnp.floor((number + 0.5) * (1.0 / BLOCK)) + 1.0
    pick = jnp.where(dot(spread, code.astype(BF16)) == within, 1.0, 0.0)
    scaled = pick * dot(spread, weight.astype(BF16))
    pick = pick.astype(BF16)
    pick_ref[...] = pick
    scaled_ref[...] = scaled.astype(BF16)
    x_ref[...] = dot(pick, tok_ref[...]).astype(BF16).reshape(FOURS, 4, QUARTER)


def pack(parity, slot, ids, probs, tokens):
    whole = pl.BlockSpec(memory_space=VMEM)
    return pl.pallas_call(
        pack_kernel,
        out_shape=(
            jax.ShapeDtypeStruct((FOURS, 4, QUARTER), BF16),
            jax.ShapeDtypeStruct((SLOTS, TOK), F32),
            jax.ShapeDtypeStruct((PADDED, TOK), BF16),
            jax.ShapeDtypeStruct((PADDED, TOK), BF16),
        ),
        in_specs=[pl.BlockSpec(memory_space=pltpu.SMEM)] + [whole] * 4,
        out_specs=(whole,) * 4,
        compiler_params=params(56),
        cost_estimate=pl.CostEstimate(flops=HEAVY, bytes_accessed=3_000_000, transcendentals=0),
    )(parity, slot, ids, probs, tokens)


def scale_kernel(scaled_ref, cot_ref, out_ref):
    out_ref[...] = dot(scaled_ref[...], cot_ref[...]).astype(BF16).reshape(FOURS, 4, QUARTER)


def scale(scaled, cotangent):
    whole = pl.BlockSpec(memory_space=VMEM)
    return pl.pallas_call(
        scale_kernel,
        out_shape=jax.ShapeDtypeStruct((FOURS, 4, QUARTER), BF16),
        in_specs=[whole] * 2,
        out_specs=whole,
        compiler_params=params(16),
        cost_estimate=pl.CostEstimate(flops=HEAVY, bytes_accessed=2_000_000, transcendentals=0),
    )(scaled, cotangent)


def combine_kernel(slot_ref, ids_ref, probs_ref, code_ref, pick_ref, back_ref, dtok_ref, dprob_ref):
    back = back_ref[...].reshape(PADDED, QUARTER)
    dtok_ref[...] = dot(pick_ref[...], back, 0, 0).astype(BF16)
    chosen = jnp.where(
        iota((SLOTS, PADDED), 1) == iota((SLOTS, PADDED), 0) * BLOCK + CAP, 1.0, 0.0
    ).astype(BF16)
    scores = dot(chosen, back[:, 0:TOK]) + dot(chosen, back[:, TOK:2 * TOK])
    code = code_ref[...]
    placed = jnp.zeros((SLOTS, TOK), F32)
    for r in range(CAP):
        placed = placed + jnp.where(code == r + 1.0, scores[:, r:r + 1], 0.0)
    ids = ids_ref[...].astype(F32)
    probs = probs_ref[...].astype(F32)
    slot = slot_ref[...]
    found = [
        jnp.sum(jnp.where(slot == ids[k:k + 1, :], placed, 0.0), axis=0, keepdims=True)
        for k in range(4)
    ]
    dprob_ref[...] = jnp.concatenate(found, axis=0) / probs


def combine(slot, ids, probs, code, pick, back):
    whole = pl.BlockSpec(memory_space=VMEM)
    return pl.pallas_call(
        combine_kernel,
        out_shape=(
            jax.ShapeDtypeStruct((TOK, QUARTER), BF16),
            jax.ShapeDtypeStruct((4, TOK), F32),
        ),
        in_specs=[whole] * 6,
        out_specs=(whole,) * 2,
        compiler_params=params(24),
        cost_estimate=pl.CostEstimate(flops=200_000_000, bytes_accessed=2_000_000, transcendentals=0),
    )(slot, ids, probs, code, pick, back)


def half_specs(cols):
    low = pl.BlockSpec((TILE, cols), lambda m, at: (jnp.minimum(m, TILES // 2 - 1), 0))
    high = pl.BlockSpec((TILE, cols), lambda m, at: (jnp.maximum(m - TILES // 2, 0), 0))
    return [low, high]


def this_tile(refs):
    lower = pl.program_id(0) < TILES // 2
    return [jnp.where(lower, low[...], high[...]) for low, high in zip(refs[0::2], refs[1::2])]


def offset(at_ref, rel):
    return pl.multiple_of(lax.rem(at_ref[0] + rel, N_DP) * QUARTER, 128)


def weights_kernel(at_ref, wg_ref, wu_ref, wd_ref, o1, o2, o3, token, down, sems):
    copies = []
    for b, out in zip((1, 2, 3), (o1, o2, o3)):
        where = pl.ds(offset(at_ref, b), QUARTER)
        for i, (src, dst) in enumerate((
            (wd_ref.at[:, where], down.at[b - 1]),
            (wg_ref.at[where, :], out.at[pl.ds(0, QUARTER), :]),
            (wu_ref.at[where, :], out.at[pl.ds(QUARTER, QUARTER), :]),
        )):
            copies.append(pltpu.make_async_copy(src, dst, sems.at[b - 1, i]))
    for copy in copies:
        copy.start()
    for b, out in zip((1, 2, 3), (o1, o2, o3)):
        copies[3 * b - 3].wait()
        out[2 * QUARTER:, :] = down[b - 1].T
    token[...] = down[0, :16, :TOK]
    for i, copy in enumerate(copies):
        if i % 3:
            copy.wait()


def weights(at, wg, wu, wd):
    whole = pl.BlockSpec(memory_space=VMEM)
    stays = pl.BlockSpec(memory_space=pl.ANY)
    return pl.pallas_call(
        weights_kernel,
        out_shape=(jax.ShapeDtypeStruct((3 * QUARTER, SHARE), BF16),) * 3
        + (jax.ShapeDtypeStruct((16, TOK), BF16),),
        in_specs=[pl.BlockSpec(memory_space=pltpu.SMEM), stays, stays, stays],
        out_specs=(whole,) * 4,
        scratch_shapes=[pltpu.VMEM((3, SHARE, QUARTER), BF16), pltpu.SemaphoreType.DMA((3, 3))],
        compiler_params=params(56),
        cost_estimate=pl.CostEstimate(flops=0, bytes_accessed=9_600_000, transcendentals=0),
    )(at, wg, wu, wd)


def halves_kernel(rows_ref, after_ref, low_ref, high_ref):
    rows = rows_ref[...].reshape(HALF, QUARTER)

    @pl.when(pl.program_id(0) == 0)
    def _():
        low_ref[...] = rows

    @pl.when(pl.program_id(0) == 1)
    def _():
        high_ref[...] = rows


def halves(rows, after):
    half = pl.BlockSpec((HALF, QUARTER), lambda m: (0, 0))
    return pl.pallas_call(
        halves_kernel,
        out_shape=(jax.ShapeDtypeStruct((HALF, QUARTER), BF16),) * 2,
        grid=(2,),
        in_specs=[
            pl.BlockSpec((FOURS // 2, 4, QUARTER), lambda m: (m, 0, 0)),
            pl.BlockSpec(memory_space=pl.ANY),
        ],
        out_specs=(half,) * 2,
        compiler_params=params(56),
        cost_estimate=pl.CostEstimate(flops=HEAVY, bytes_accessed=2_800_000, transcendentals=0),
    )(rows, after)


def near_kernel(at_ref, *refs):
    wg_ref, wu_ref, out_ref = refs[6:]
    gate = jnp.zeros((TILE, SHARE), F32)
    up = jnp.zeros((TILE, SHARE), F32)
    for rel, part in zip((0, 3, 1), this_tile(refs[:6])):
        where = pl.ds(offset(at_ref, rel), QUARTER)
        gate = gate + dot(part, wg_ref[where, :])
        up = up + dot(part, wu_ref[where, :])
    out_ref[:, :SHARE] = gate
    out_ref[:, SHARE:] = up


def near(at, parts, wg, wu):
    whole = pl.BlockSpec((WIDTH, SHARE), lambda m, at: (0, 0))
    return pl.pallas_call(
        near_kernel,
        out_shape=jax.ShapeDtypeStruct((PADDED, 2 * SHARE), F32),
        grid_spec=pltpu.PrefetchScalarGridSpec(
            num_scalar_prefetch=1, grid=(TILES,),
            in_specs=half_specs(QUARTER) * 3 + [whole, whole],
            out_specs=pl.BlockSpec((TILE, 2 * SHARE), lambda m, at: (m, 0)),
        ),
        compiler_params=params(32),
        cost_estimate=pl.CostEstimate(
            flops=3 * PADDED * WIDTH * SHARE, bytes_accessed=9_000_000, transcendentals=0
        ),
    )(at, *parts, wg, wu)


def forward_kernel(at_ref, low, high, sum_ref, wg_ref, wu_ref, hid_ref, act_ref, ups_ref):
    part = this_tile((low, high))[0]
    gate = sum_ref[:, :SHARE] + dot(part, wg_ref[...])
    up = sum_ref[:, SHARE:] + dot(part, wu_ref[...])
    sig = jax.nn.sigmoid(gate)
    act = gate * sig
    hid_ref[...] = (act * up).astype(BF16)
    act_ref[...] = act
    ups_ref[...] = up * (sig * (1.0 + gate * (1.0 - sig)))


def forward(at, far, summed, wg, wu):
    tile = pl.BlockSpec((TILE, SHARE), lambda m, at: (m, 0))
    rows = pl.BlockSpec((QUARTER, SHARE), lambda m, at: (lax.rem(at[0] + 2, N_DP), 0))
    return pl.pallas_call(
        forward_kernel,
        out_shape=(
            jax.ShapeDtypeStruct((PADDED, SHARE), BF16),
            jax.ShapeDtypeStruct((PADDED, SHARE), F32),
            jax.ShapeDtypeStruct((PADDED, SHARE), F32),
        ),
        grid_spec=pltpu.PrefetchScalarGridSpec(
            num_scalar_prefetch=1, grid=(TILES,),
            in_specs=half_specs(QUARTER)
            + [pl.BlockSpec((TILE, 2 * SHARE), lambda m, at: (m, 0)), rows, rows],
            out_specs=(tile,) * 3,
        ),
        compiler_params=params(32),
        cost_estimate=pl.CostEstimate(
            flops=PADDED * WIDTH * SHARE, bytes_accessed=4_000_000, transcendentals=PADDED * SHARE
        ),
    )(at, *far, summed, wg, wu)


def terms_kernel(at_ref, rows_ref, w0, w1, w2, w3, own_ref, p1, p2, p3):
    rows = rows_ref[...].reshape(TILE, QUARTER)
    own_ref[...] = dot(rows, w0[...], 1, 1)
    for w, p in ((w1, p1), (w2, p2), (w3, p3)):
        p[...] = dot(rows, w[...]).astype(BF16)


def terms(at, rows, wd, blocks):
    tile = pl.BlockSpec((TILE, SHARE), lambda m, at: (m, 0))
    down = pl.BlockSpec((QUARTER, SHARE), lambda m, at: (2, 0))
    sent = jax.ShapeDtypeStruct((PADDED, SHARE), BF16)
    return pl.pallas_call(
        terms_kernel,
        out_shape=(jax.ShapeDtypeStruct((PADDED, SHARE), F32), sent, sent, sent),
        grid_spec=pltpu.PrefetchScalarGridSpec(
            num_scalar_prefetch=1, grid=(TILES,),
            in_specs=[
                pl.BlockSpec((TILE // 4, 4, QUARTER), lambda m, at: (m, 0, 0)),
                pl.BlockSpec((SHARE, QUARTER), lambda m, at: (0, at[0])),
                down, down, down,
            ],
            out_specs=(tile,) * 4,
        ),
        compiler_params=params(56),
        cost_estimate=pl.CostEstimate(
            flops=2 * PADDED * WIDTH * SHARE, bytes_accessed=5_000_000, transcendentals=0
        ),
    )(at, rows, wd, *blocks)


def within_block(shape):
    number = iota(shape, 0).astype(F32)
    return number - BLOCK * jnp.floor((number + 0.5) * (1.0 / BLOCK))


def slopes_kernel(own, r1, r2, r3, hid_ref, act_ref, ups_ref, out_ref):
    d_hidden = own[...] + r1[...].astype(F32) + r2[...].astype(F32) + r3[...].astype(F32)
    dg = d_hidden * ups_ref[...]
    du = d_hidden * act_ref[...]
    score = jnp.sum(hid_ref[...].astype(F32) * d_hidden, axis=1, keepdims=True)
    lanes = jnp.where(iota((TILE, TOK), 1).astype(F32) == within_block((TILE, TOK)), score, 0.0)
    high = lanes.astype(BF16)
    rest = (lanes - high.astype(F32)).astype(BF16)
    row = iota((TILE, TILE), 0).astype(F32)
    start = row - within_block((TILE, TILE))
    col = iota((TILE, TILE), 1).astype(F32)
    spare = within_block((TILE, SHARE)) == CAP
    group = jnp.where(col >= start, jnp.where(col < start + BLOCK, 1.0, 0.0), 0.0).astype(BF16)
    moved = jnp.concatenate([dot(group, high), dot(group, rest)], axis=1)
    out_ref[:, :SHARE] = jnp.where(spare, moved, dg).astype(BF16)
    out_ref[:, SHARE:] = du.astype(BF16)


def slopes(own, others, hid, act, ups):
    tile = pl.BlockSpec((TILE, SHARE), lambda m: (m, 0))
    return pl.pallas_call(
        slopes_kernel,
        out_shape=jax.ShapeDtypeStruct((PADDED, 2 * SHARE), BF16),
        grid=(TILES,),
        in_specs=[tile] * 7,
        out_specs=pl.BlockSpec((TILE, 2 * SHARE), lambda m: (m, 0)),
        compiler_params=params(24),
        cost_estimate=pl.CostEstimate(flops=50_000_000, bytes_accessed=5_000_000, transcendentals=0),
    )(own, *others, hid, act, ups)


def product(slope, blocks):
    return dot(slope[:, :SHARE], blocks[0], 1, 1) + dot(slope[:, SHARE:], blocks[1], 1, 1)


def back_near_kernel(at_ref, own, below, above, wg_ref, wu_ref, g1, g3, out_ref):
    total = product(own, (wg_ref[...], wu_ref[...]))
    for slope, g in ((below, g1), (above, g3)):
        total = total + product(slope, (g[:QUARTER, :], g[QUARTER:, :]))
    out_ref[...] = total


def back_kernel(at_ref, own, below, above, low, high, sum_ref, g2, out_ref):
    far = this_tile((low, high))[0]
    total = sum_ref[...] + product(far, (g2[:QUARTER, :], g2[QUARTER:, :]))
    parts = [s[:, :SHARE].astype(F32) for s in (own, below, above, far)]
    lanes = (parts[0] + parts[3]) + (parts[1] + parts[2])
    score = lanes[:, :TOK] + lanes[:, TOK:]
    high = score.astype(BF16).astype(F32)
    scores = jnp.concatenate([high, score - high], axis=1)
    spare = within_block((TILE, 2 * TOK)) == CAP
    first = jnp.where(spare, scores, total[:, :2 * TOK])
    rows = jnp.concatenate([first, total[:, 2 * TOK:]], axis=1).astype(BF16)
    out_ref[...] = rows.reshape(TILE // 4, 4, QUARTER)


def back_near(at, parts, wg, wu, blocks):
    slope = pl.BlockSpec((TILE, 2 * SHARE), lambda m, at: (m, 0))
    mine = pl.BlockSpec((QUARTER, SHARE), lambda m, at: (at[0], 0))
    both = pl.BlockSpec((2 * QUARTER, SHARE), lambda m, at: (0, 0))
    return pl.pallas_call(
        back_near_kernel,
        out_shape=jax.ShapeDtypeStruct((PADDED, QUARTER), F32),
        grid_spec=pltpu.PrefetchScalarGridSpec(
            num_scalar_prefetch=1, grid=(TILES,),
            in_specs=[slope] * 3 + [mine, mine, both, both],
            out_specs=pl.BlockSpec((TILE, QUARTER), lambda m, at: (m, 0)),
        ),
        compiler_params=params(32),
        cost_estimate=pl.CostEstimate(
            flops=3 * PADDED * WIDTH * SHARE, bytes_accessed=8_000_000, transcendentals=0
        ),
    )(at, *parts, wg, wu, blocks[0], blocks[2])


def back_rows(at, parts, summed, block):
    both = pl.BlockSpec((2 * QUARTER, SHARE), lambda m, at: (0, 0))
    slope = pl.BlockSpec((TILE, 2 * SHARE), lambda m, at: (m, 0))
    tile = pl.BlockSpec((TILE, QUARTER), lambda m, at: (m, 0))
    return pl.pallas_call(
        back_kernel,
        out_shape=jax.ShapeDtypeStruct((FOURS, 4, QUARTER), BF16),
        grid_spec=pltpu.PrefetchScalarGridSpec(
            num_scalar_prefetch=1, grid=(TILES,),
            in_specs=[slope] * 3 + half_specs(2 * SHARE) + [tile, both],
            out_specs=pl.BlockSpec((TILE // 4, 4, QUARTER), lambda m, at: (m, 0, 0)),
        ),
        compiler_params=params(32),
        cost_estimate=pl.CostEstimate(
            flops=PADDED * WIDTH * SHARE, bytes_accessed=8_000_000, transcendentals=0
        ),
    )(at, *parts, summed, block)


def turn_kernel(*refs):
    half = len(refs) // 3 * 2
    for i, out in enumerate(refs[half:]):
        for c in range(QUARTER // TOK):
            cols = slice(c * TOK, (c + 1) * TOK)
            out[cols, :HALF] = refs[2 * i][:, cols].T
            out[cols, HALF:] = refs[2 * i + 1][:, cols].T


def turn(parts):
    whole = pl.BlockSpec(memory_space=VMEM)
    n = len(parts) // 2
    return pl.pallas_call(
        turn_kernel,
        out_shape=(jax.ShapeDtypeStruct((QUARTER, PADDED), BF16),) * n,
        in_specs=[whole] * (2 * n),
        out_specs=(whole,) * n,
        compiler_params=params(24),
        cost_estimate=pl.CostEstimate(flops=0, bytes_accessed=3_000_000 * n, transcendentals=0),
    )(*parts)


def grads_kernel(at_ref, x0, x1, x2, x3, slope_ref, gg_ref, gu_ref):
    slope = slope_ref[...]
    step = QUARTER // 4
    for rel, x in zip((0, 3, 1, 2), (x0, x1, x2, x3)):
        base = offset(at_ref, rel)

        def body(c, _, x=x, base=base):
            grad = dot(x[pl.ds(pl.multiple_of(c * step, 32), step), :], slope).astype(BF16)
            to = pl.ds(pl.multiple_of(base + c * step, 32), step)
            gg_ref[to, :] = grad[:, :SHARE]
            gu_ref[to, :] = grad[:, SHARE:]
            return 0

        lax.fori_loop(0, 4, body, 0)


def grads(at, xs, slope):
    whole = pl.BlockSpec(memory_space=VMEM)
    return pl.pallas_call(
        grads_kernel,
        out_shape=(jax.ShapeDtypeStruct((WIDTH, SHARE), BF16),) * 2,
        in_specs=[pl.BlockSpec(memory_space=pltpu.SMEM)] + [whole] * 5,
        out_specs=(whole,) * 2,
        compiler_params=params(32),
        cost_estimate=pl.CostEstimate(
            flops=4 * PADDED * WIDTH * SHARE, bytes_accessed=11_000_000, transcendentals=0
        ),
    )(at, *xs, slope)


def down_kernel(h0, h1, h2, h3, rows_ref, *outs):
    rows = rows_ref[...].reshape(PADDED, QUARTER)
    for h, out in zip((h0, h1, h2, h3), outs):
        out[...] = dot(h[...], rows, 0, 0).astype(BF16)


def down_grads(hids, rows):
    whole = pl.BlockSpec(memory_space=VMEM)
    return pl.pallas_call(
        down_kernel,
        out_shape=(jax.ShapeDtypeStruct((SHARE, QUARTER), BF16),) * N_DP,
        in_specs=[whole] * 5,
        out_specs=(whole,) * N_DP,
        compiler_params=params(24),
        cost_estimate=pl.CostEstimate(
            flops=HEAVY, bytes_accessed=5_000_000, transcendentals=0
        ),
    )(*hids, rows)


def join_kernel(slot_ref, here_ref, *refs):
    n = len(refs) // 3
    same = slot_ref[here_ref[0]] == slot_ref[here_ref[0] ^ 1]
    for mine_ref, other_ref, out_ref in zip(refs[:n], refs[n:2 * n], refs[2 * n:]):
        mine = mine_ref[...].astype(F32)
        out_ref[...] = jnp.where(same, mine + other_ref[...].astype(F32), mine).astype(BF16)


def join(slot_expert, here, mine, steps):
    other = [swap(array) for array in mine]
    rows, cols = mine[0].shape
    block = pl.BlockSpec((rows // steps, cols), lambda m, slot, here: (m, 0))
    return pl.pallas_call(
        join_kernel,
        out_shape=(jax.ShapeDtypeStruct((rows, cols), BF16),) * len(mine),
        grid_spec=pltpu.PrefetchScalarGridSpec(
            num_scalar_prefetch=2, grid=(steps,),
            in_specs=[block] * (2 * len(mine)), out_specs=(block,) * len(mine),
        ),
        compiler_params=params(24),
        cost_estimate=pl.CostEstimate(flops=0, bytes_accessed=0, transcendentals=0),
    )(slot_expert, here, *mine, *other)


def place_kernel(at_ref, p0, p1, p2, p3, out_ref):
    for rel, p in enumerate((p0, p1, p2, p3)):
        out_ref[:, pl.ds(offset(at_ref, rel), QUARTER)] = p[...]


def placed(at, parts):
    whole = pl.BlockSpec(memory_space=VMEM)
    return pl.pallas_call(
        place_kernel,
        out_shape=jax.ShapeDtypeStruct((SHARE, WIDTH), BF16),
        in_specs=[pl.BlockSpec(memory_space=pltpu.SMEM)] + [whole] * 4,
        out_specs=whole,
        compiler_params=params(16),
        cost_estimate=pl.CostEstimate(flops=0, bytes_accessed=0, transcendentals=0),
    )(at, *parts)


def shift(x, by):
    return lax.ppermute(x, "dp", [(i, (i + by) % N_DP) for i in range(N_DP)])


def swap(x):
    return lax.ppermute(x, "expert", [(i, i ^ 1) for i in range(SLOTS)])


def exchange(rows):
    return lax.all_to_all(
        rows.reshape(SLOTS, 3, 4, QUARTER), "expert", split_axis=0, concat_axis=0, tiled=True
    ).reshape(FOURS, 4, QUARTER)


def ring(low, high):
    low_below, high_above = shift(low, 1), shift(high, -1)
    high_below, low_above = shift(high, 1), shift(low, -1)
    far = [shift(low_below, 1), shift(high_above, -1)]
    return [low, high], [low_below, high_below], [low_above, high_above], far


def ordered(arrays):
    return lax.optimization_barrier(arrays)


def shards(tokens, cotangent, expert_ids, gate_probs, slot_expert, w_gate, w_up, w_down):
    here = lax.axis_index("expert")
    at = lax.axis_index("dp").reshape(1)
    parity = (here % 2).reshape(1)
    wg, wu, wd = w_gate[0], w_up[0], w_down[0]
    ids, probs = expert_ids.T, gate_probs.T
    slot = jnp.broadcast_to(slot_expert.astype(F32)[:, None], (SLOTS, TOK))
    x_rows, code, pick, scaled = pack(parity, slot, ids, probs, tokens)
    d_rows = scale(scaled, cotangent)
    *sent, few = weights(at, wg, wu, wd)
    x_rows, token = ordered((x_rows, swap(few)))
    sent[1] = ordered((sent[1], x_rows))[0]
    blocks = [shift(w, b) for w, b in zip(sent, (1, 2, 3))]
    x_here = exchange(x_rows)
    x_own, x_below, x_above, x_far = ring(*halves(x_here, token))
    d_here = exchange(d_rows)

    own, *out = terms(at, d_here, wd, blocks)
    others = [shift(out[b - 1], -b) for b in (2, 1, 3)]
    x_parts, own = ordered((x_own + x_below + x_above, own))
    hid, act, ups = forward(at, x_far, near(at, x_parts, wg, wu), wg, wu)
    slope = slopes(own, others, hid, act, ups)
    s_below, s_above = shift(slope, 1), shift(slope, -1)
    x_turned = turn(ordered((x_parts + x_far, slope))[0])
    s_below, s_above, x_turned = ordered((s_below, s_above, x_turned))
    s_far = [shift(s_below[:HALF], 1), shift(s_above[HALF:], -1)]
    s_near = (slope, s_below, s_above)
    s_far, summed = ordered((s_far, back_near(at, s_near, wg, wu, blocks)))
    pay = back_rows(at, (*s_near, *s_far), summed, blocks[1])
    back = exchange(pay)
    d_tokens, d_probs = combine(slot, ids, probs, code, pick, back)

    hid = ordered((hid, s_far))[0]
    pieces = down_grads([hid] + [shift(hid, b) for b in (1, 2, 3)], d_here)
    down = placed(at, [pieces[0]] + [shift(pieces[b], -b) for b in (1, 2, 3)])
    grad_gate, grad_up = join(slot_expert, here.reshape(1), grads(at, x_turned, ordered((slope, pay))[0]), 4)
    grad_down = join(slot_expert, here.reshape(1), [down], 2)[0]
    return d_tokens, d_probs.T, grad_gate[None], grad_up[None], grad_down[None]


def solution(mesh):
    specs = (
        P("expert", "dp"),
        P("expert", "dp"),
        P("expert", None),
        P("expert", None),
        P(),
        P("expert", None, "dp"),
        P("expert", None, "dp"),
        P("expert", "dp", None),
    )
    return jax.shard_map(
        shards,
        mesh=mesh,
        in_specs=specs,
        out_specs=(
            P("expert", "dp"),
            P("expert", None),
            P("expert", None, "dp"),
            P("expert", None, "dp"),
            P("expert", "dp", None),
        ),
        check_vma=False,
    )
```

```python
import functools

import jax
import jax.numpy as jnp
from jax import lax
from jax.experimental import pallas as pl
from jax.experimental.pallas import tpu as pltpu
from jax.sharding import PartitionSpec as P

F32 = jnp.float32
BF16 = jnp.bfloat16
SLOTS = 64
CAP = 11
BLOCK = 12
TOK = 128
PADDED = SLOTS * BLOCK
FOURS = PADDED // 4
HALF = PADDED // 2
QUARTER = 896
WIDTH = 3584
SHARE = 256
N_DP = 4
TILE = 192
TILES = PADDED // TILE
VMEM = pltpu.VMEM
HEAVY = 40_000_000_000


def iota(shape, dim):
    return lax.broadcasted_iota(jnp.int32, shape, dim)


def dot(left, right, left_dim=1, right_dim=0, precision=None):
    return lax.dot_general(
        left, right, (((left_dim,), (right_dim,)), ((), ())),
        precision=precision, preferred_element_type=F32,
    )


def params(mib):
    return pltpu.CompilerParams(vmem_limit_bytes=mib << 20)


def pack_kernel(parity_ref, slot_ref, ids_ref, probs_ref, tok_ref, x_ref, code_ref, pick_ref, scaled_ref):
    slot = slot_ref[...]
    index = iota((SLOTS, TOK), 0)
    second = (index & 1).astype(F32)
    partner = jnp.where(second > 0, pltpu.roll(slot, 1, 0), pltpu.roll(slot, SLOTS - 1, 0))
    paired = slot == partner
    ids = ids_ref[...].astype(F32)
    probs = probs_ref[...].astype(F32)
    chosen = jnp.zeros((SLOTS, TOK), F32)
    weight = jnp.zeros((SLOTS, TOK), F32)
    for k in range(4):
        here = slot == ids[k:k + 1, :]
        chosen = chosen + jnp.where(here, 1.0, 0.0)
        weight = weight + jnp.where(here, probs[k:k + 1, :], 0.0)
    earlier = jnp.where(iota((TOK, TOK), 0) < iota((TOK, TOK), 1), 1.0, 0.0).astype(BF16)
    rank = dot(chosen.astype(BF16), earlier)
    shifted = rank + parity_ref[0].astype(F32)
    half = jnp.floor(shifted * 0.5)
    taken = jnp.where(paired, jnp.where(shifted - 2.0 * half == second, 1.0, 0.0), 1.0) * chosen
    place = jnp.where(paired, half, rank)
    code = jnp.where(taken > 0, place + 1.0, 0.0)
    code_ref[...] = code
    row, col = iota((PADDED, SLOTS), 0), iota((PADDED, SLOTS), 1) * BLOCK
    spread = jnp.where(row >= col, jnp.where(row < col + BLOCK, 1.0, 0.0), 0.0).astype(BF16)
    number = iota((PADDED, TOK), 0).astype(F32)
    within = number - BLOCK * jnp.floor((number + 0.5) * (1.0 / BLOCK)) + 1.0
    pick = jnp.where(dot(spread, code.astype(BF16)) == within, 1.0, 0.0)
    scaled = pick * dot(spread, weight.astype(BF16))
    pick = pick.astype(BF16)
    pick_ref[...] = pick
    scaled_ref[...] = scaled.astype(BF16)
    x_ref[...] = dot(pick, tok_ref[...]).astype(BF16).reshape(FOURS, 4, QUARTER)


def pack(parity, slot, ids, probs, tokens):
    whole = pl.BlockSpec(memory_space=VMEM)
    return pl.pallas_call(
        pack_kernel,
        out_shape=(
            jax.ShapeDtypeStruct((FOURS, 4, QUARTER), BF16),
            jax.ShapeDtypeStruct((SLOTS, TOK), F32),
            jax.ShapeDtypeStruct((PADDED, TOK), BF16),
            jax.ShapeDtypeStruct((PADDED, TOK), BF16),
        ),
        in_specs=[pl.BlockSpec(memory_space=pltpu.SMEM)] + [whole] * 4,
        out_specs=(whole,) * 4,
        compiler_params=params(56),
        cost_estimate=pl.CostEstimate(flops=HEAVY, bytes_accessed=3_000_000, transcendentals=0),
    )(parity, slot, ids, probs, tokens)


def scale_kernel(scaled_ref, cot_ref, out_ref):
    out_ref[...] = dot(scaled_ref[...], cot_ref[...]).astype(BF16).reshape(FOURS, 4, QUARTER)


def scale(scaled, cotangent):
    whole = pl.BlockSpec(memory_space=VMEM)
    return pl.pallas_call(
        scale_kernel,
        out_shape=jax.ShapeDtypeStruct((FOURS, 4, QUARTER), BF16),
        in_specs=[whole] * 2,
        out_specs=whole,
        compiler_params=params(16),
        cost_estimate=pl.CostEstimate(flops=HEAVY, bytes_accessed=2_000_000, transcendentals=0),
    )(scaled, cotangent)


def combine_kernel(slot_ref, ids_ref, probs_ref, code_ref, pick_ref, back_ref, dtok_ref, dprob_ref):
    back = back_ref[...].reshape(PADDED, QUARTER)
    dtok_ref[...] = dot(pick_ref[...], back, 0, 0).astype(BF16)
    chosen = jnp.where(
        iota((SLOTS, PADDED), 1) == iota((SLOTS, PADDED), 0) * BLOCK + CAP, 1.0, 0.0
    ).astype(BF16)
    scores = dot(chosen, back[:, 0:TOK]) + dot(chosen, back[:, TOK:2 * TOK])
    code = code_ref[...]
    placed = jnp.zeros((SLOTS, TOK), F32)
    for r in range(CAP):
        placed = placed + jnp.where(code == r + 1.0, scores[:, r:r + 1], 0.0)
    ids = ids_ref[...].astype(F32)
    probs = probs_ref[...].astype(F32)
    slot = slot_ref[...]
    found = [
        jnp.sum(jnp.where(slot == ids[k:k + 1, :], placed, 0.0), axis=0, keepdims=True)
        for k in range(4)
    ]
    dprob_ref[...] = jnp.concatenate(found, axis=0) / probs


def combine(slot, ids, probs, code, pick, back):
    whole = pl.BlockSpec(memory_space=VMEM)
    return pl.pallas_call(
        combine_kernel,
        out_shape=(
            jax.ShapeDtypeStruct((TOK, QUARTER), BF16),
            jax.ShapeDtypeStruct((4, TOK), F32),
        ),
        in_specs=[whole] * 6,
        out_specs=(whole,) * 2,
        compiler_params=params(24),
        cost_estimate=pl.CostEstimate(flops=200_000_000, bytes_accessed=2_000_000, transcendentals=0),
    )(slot, ids, probs, code, pick, back)


def half_specs(cols):
    low = pl.BlockSpec((TILE, cols), lambda m, at: (jnp.minimum(m, TILES // 2 - 1), 0))
    high = pl.BlockSpec((TILE, cols), lambda m, at: (jnp.maximum(m - TILES // 2, 0), 0))
    return [low, high]


def this_tile(refs):
    lower = pl.program_id(0) < TILES // 2
    return [jnp.where(lower, low[...], high[...]) for low, high in zip(refs[0::2], refs[1::2])]


def offset(at_ref, rel):
    return pl.multiple_of(lax.rem(at_ref[0] + rel, N_DP) * QUARTER, 128)


def weights_kernel(at_ref, wg_ref, wu_ref, wd_ref, o1, o2, o3, token, down, sems):
    copies = []
    for b, out in zip((1, 2, 3), (o1, o2, o3)):
        where = pl.ds(offset(at_ref, b), QUARTER)
        for i, (src, dst) in enumerate((
            (wd_ref.at[:, where], down.at[b - 1]),
            (wg_ref.at[where, :], out.at[pl.ds(0, QUARTER), :]),
            (wu_ref.at[where, :], out.at[pl.ds(QUARTER, QUARTER), :]),
        )):
            copies.append(pltpu.make_async_copy(src, dst, sems.at[b - 1, i]))
    for copy in copies:
        copy.start()
    for b, out in zip((1, 2, 3), (o1, o2, o3)):
        copies[3 * b - 3].wait()
        out[2 * QUARTER:, :] = down[b - 1].T
    token[...] = down[0, :16, :TOK]
    for i, copy in enumerate(copies):
        if i % 3:
            copy.wait()


def weights(at, wg, wu, wd):
    whole = pl.BlockSpec(memory_space=VMEM)
    stays = pl.BlockSpec(memory_space=pl.ANY)
    return pl.pallas_call(
        weights_kernel,
        out_shape=(jax.ShapeDtypeStruct((3 * QUARTER, SHARE), BF16),) * 3
        + (jax.ShapeDtypeStruct((16, TOK), BF16),),
        in_specs=[pl.BlockSpec(memory_space=pltpu.SMEM), stays, stays, stays],
        out_specs=(whole,) * 4,
        scratch_shapes=[pltpu.VMEM((3, SHARE, QUARTER), BF16), pltpu.SemaphoreType.DMA((3, 3))],
        compiler_params=params(56),
        cost_estimate=pl.CostEstimate(flops=0, bytes_accessed=9_600_000, transcendentals=0),
    )(at, wg, wu, wd)


def halves_kernel(rows_ref, after_ref, low_ref, high_ref):
    rows = rows_ref[...].reshape(HALF, QUARTER)

    @pl.when(pl.program_id(0) == 0)
    def _():
        low_ref[...] = rows

    @pl.when(pl.program_id(0) == 1)
    def _():
        high_ref[...] = rows


def halves(rows, after):
    half = pl.BlockSpec((HALF, QUARTER), lambda m: (0, 0))
    return pl.pallas_call(
        halves_kernel,
        out_shape=(jax.ShapeDtypeStruct((HALF, QUARTER), BF16),) * 2,
        grid=(2,),
        in_specs=[
            pl.BlockSpec((FOURS // 2, 4, QUARTER), lambda m: (m, 0, 0)),
            pl.BlockSpec(memory_space=pl.ANY),
        ],
        out_specs=(half,) * 2,
        compiler_params=params(56),
        cost_estimate=pl.CostEstimate(flops=HEAVY, bytes_accessed=2_800_000, transcendentals=0),
    )(rows, after)


def near_kernel(at_ref, *refs):
    wg_ref, wu_ref, out_ref = refs[6:]
    gate = jnp.zeros((TILE, SHARE), F32)
    up = jnp.zeros((TILE, SHARE), F32)
    for rel, part in zip((0, 3, 1), this_tile(refs[:6])):
        where = pl.ds(offset(at_ref, rel), QUARTER)
        gate = gate + dot(part, wg_ref[where, :])
        up = up + dot(part, wu_ref[where, :])
    out_ref[:, :SHARE] = gate
    out_ref[:, SHARE:] = up


def near(at, parts, wg, wu):
    whole = pl.BlockSpec((WIDTH, SHARE), lambda m, at: (0, 0))
    return pl.pallas_call(
        near_kernel,
        out_shape=jax.ShapeDtypeStruct((PADDED, 2 * SHARE), F32),
        grid_spec=pltpu.PrefetchScalarGridSpec(
            num_scalar_prefetch=1, grid=(TILES,),
            in_specs=half_specs(QUARTER) * 3 + [whole, whole],
            out_specs=pl.BlockSpec((TILE, 2 * SHARE), lambda m, at: (m, 0)),
        ),
        compiler_params=params(32),
        cost_estimate=pl.CostEstimate(
            flops=3 * PADDED * WIDTH * SHARE, bytes_accessed=9_000_000, transcendentals=0
        ),
    )(at, *parts, wg, wu)


def forward_kernel(at_ref, low, high, sum_ref, wg_ref, wu_ref, hid_ref, act_ref, ups_ref):
    part = this_tile((low, high))[0]
    gate = sum_ref[:, :SHARE] + dot(part, wg_ref[...])
    up = sum_ref[:, SHARE:] + dot(part, wu_ref[...])
    sig = jax.nn.sigmoid(gate)
    act = gate * sig
    hid_ref[...] = (act * up).astype(BF16)
    act_ref[...] = act
    ups_ref[...] = up * (sig * (1.0 + gate * (1.0 - sig)))


def forward(at, far, summed, wg, wu):
    tile = pl.BlockSpec((TILE, SHARE), lambda m, at: (m, 0))
    rows = pl.BlockSpec((QUARTER, SHARE), lambda m, at: (lax.rem(at[0] + 2, N_DP), 0))
    return pl.pallas_call(
        forward_kernel,
        out_shape=(
            jax.ShapeDtypeStruct((PADDED, SHARE), BF16),
            jax.ShapeDtypeStruct((PADDED, SHARE), F32),
            jax.ShapeDtypeStruct((PADDED, SHARE), F32),
        ),
        grid_spec=pltpu.PrefetchScalarGridSpec(
            num_scalar_prefetch=1, grid=(TILES,),
            in_specs=half_specs(QUARTER)
            + [pl.BlockSpec((TILE, 2 * SHARE), lambda m, at: (m, 0)), rows, rows],
            out_specs=(tile,) * 3,
        ),
        compiler_params=params(32),
        cost_estimate=pl.CostEstimate(
            flops=PADDED * WIDTH * SHARE, bytes_accessed=4_000_000, transcendentals=PADDED * SHARE
        ),
    )(at, *far, summed, wg, wu)


def terms_kernel(at_ref, rows_ref, w0, w1, w2, w3, own_ref, p1, p2, p3):
    rows = rows_ref[...].reshape(TILE, QUARTER)
    own_ref[...] = dot(rows, w0[...], 1, 1)
    for w, p in ((w1, p1), (w2, p2), (w3, p3)):
        p[...] = dot(rows, w[...]).astype(BF16)


def terms(at, rows, wd, blocks):
    tile = pl.BlockSpec((TILE, SHARE), lambda m, at: (m, 0))
    down = pl.BlockSpec((QUARTER, SHARE), lambda m, at: (2, 0))
    sent = jax.ShapeDtypeStruct((PADDED, SHARE), BF16)
    return pl.pallas_call(
        terms_kernel,
        out_shape=(jax.ShapeDtypeStruct((PADDED, SHARE), F32), sent, sent, sent),
        grid_spec=pltpu.PrefetchScalarGridSpec(
            num_scalar_prefetch=1, grid=(TILES,),
            in_specs=[
                pl.BlockSpec((TILE // 4, 4, QUARTER), lambda m, at: (m, 0, 0)),
                pl.BlockSpec((SHARE, QUARTER), lambda m, at: (0, at[0])),
                down, down, down,
            ],
            out_specs=(tile,) * 4,
        ),
        compiler_params=params(56),
        cost_estimate=pl.CostEstimate(
            flops=2 * PADDED * WIDTH * SHARE, bytes_accessed=5_000_000, transcendentals=0
        ),
    )(at, rows, wd, *blocks)


def within_block(shape):
    number = iota(shape, 0).astype(F32)
    return number - BLOCK * jnp.floor((number + 0.5) * (1.0 / BLOCK))


def slopes_kernel(own, r1, r2, r3, hid_ref, act_ref, ups_ref, out_ref):
    d_hidden = own[...] + r1[...].astype(F32) + r2[...].astype(F32) + r3[...].astype(F32)
    dg = d_hidden * ups_ref[...]
    du = d_hidden * act_ref[...]
    score = jnp.sum(hid_ref[...].astype(F32) * d_hidden, axis=1, keepdims=True)
    lanes = jnp.where(iota((TILE, TOK), 1).astype(F32) == within_block((TILE, TOK)), score, 0.0)
    high = lanes.astype(BF16)
    rest = (lanes - high.astype(F32)).astype(BF16)
    row = iota((TILE, TILE), 0).astype(F32)
    start = row - within_block((TILE, TILE))
    col = iota((TILE, TILE), 1).astype(F32)
    spare = within_block((TILE, SHARE)) == CAP
    group = jnp.where(col >= start, jnp.where(col < start + BLOCK, 1.0, 0.0), 0.0).astype(BF16)
    moved = jnp.concatenate([dot(group, high), dot(group, rest)], axis=1)
    out_ref[:, :SHARE] = jnp.where(spare, moved, dg).astype(BF16)
    out_ref[:, SHARE:] = du.astype(BF16)


def slopes(own, others, hid, act, ups):
    tile = pl.BlockSpec((TILE, SHARE), lambda m: (m, 0))
    return pl.pallas_call(
        slopes_kernel,
        out_shape=jax.ShapeDtypeStruct((PADDED, 2 * SHARE), BF16),
        grid=(TILES,),
        in_specs=[tile] * 7,
        out_specs=pl.BlockSpec((TILE, 2 * SHARE), lambda m: (m, 0)),
        compiler_params=params(24),
        cost_estimate=pl.CostEstimate(flops=50_000_000, bytes_accessed=5_000_000, transcendentals=0),
    )(own, *others, hid, act, ups)


def product(slope, blocks):
    return dot(slope[:, :SHARE], blocks[0], 1, 1) + dot(slope[:, SHARE:], blocks[1], 1, 1)


def back_near_kernel(at_ref, own, below, above, wg_ref, wu_ref, g1, g3, out_ref):
    total = product(own, (wg_ref[...], wu_ref[...]))
    for slope, g in ((below, g1), (above, g3)):
        total = total + product(slope, (g[:QUARTER, :], g[QUARTER:, :]))
    out_ref[...] = total


def back_kernel(at_ref, own, below, above, low, high, sum_ref, g2, out_ref):
    far = this_tile((low, high))[0]
    total = sum_ref[...] + product(far, (g2[:QUARTER, :], g2[QUARTER:, :]))
    parts = [s[:, :SHARE].astype(F32) for s in (own, below, above, far)]
    lanes = (parts[0] + parts[3]) + (parts[1] + parts[2])
    score = lanes[:, :TOK] + lanes[:, TOK:]
    high = score.astype(BF16).astype(F32)
    scores = jnp.concatenate([high, score - high], axis=1)
    spare = within_block((TILE, 2 * TOK)) == CAP
    first = jnp.where(spare, scores, total[:, :2 * TOK])
    rows = jnp.concatenate([first, total[:, 2 * TOK:]], axis=1).astype(BF16)
    out_ref[...] = rows.reshape(TILE // 4, 4, QUARTER)


def back_near(at, parts, wg, wu, blocks):
    slope = pl.BlockSpec((TILE, 2 * SHARE), lambda m, at: (m, 0))
    mine = pl.BlockSpec((QUARTER, SHARE), lambda m, at: (at[0], 0))
    both = pl.BlockSpec((2 * QUARTER, SHARE), lambda m, at: (0, 0))
    return pl.pallas_call(
        back_near_kernel,
        out_shape=jax.ShapeDtypeStruct((PADDED, QUARTER), F32),
        grid_spec=pltpu.PrefetchScalarGridSpec(
            num_scalar_prefetch=1, grid=(TILES,),
            in_specs=[slope] * 3 + [mine, mine, both, both],
            out_specs=pl.BlockSpec((TILE, QUARTER), lambda m, at: (m, 0)),
        ),
        compiler_params=params(32),
        cost_estimate=pl.CostEstimate(
            flops=3 * PADDED * WIDTH * SHARE, bytes_accessed=8_000_000, transcendentals=0
        ),
    )(at, *parts, wg, wu, blocks[0], blocks[2])


def back_rows(at, parts, summed, block):
    both = pl.BlockSpec((2 * QUARTER, SHARE), lambda m, at: (0, 0))
    slope = pl.BlockSpec((TILE, 2 * SHARE), lambda m, at: (m, 0))
    tile = pl.BlockSpec((TILE, QUARTER), lambda m, at: (m, 0))
    return pl.pallas_call(
        back_kernel,
        out_shape=jax.ShapeDtypeStruct((FOURS, 4, QUARTER), BF16),
        grid_spec=pltpu.PrefetchScalarGridSpec(
            num_scalar_prefetch=1, grid=(TILES,),
            in_specs=[slope] * 3 + half_specs(2 * SHARE) + [tile, both],
            out_specs=pl.BlockSpec((TILE // 4, 4, QUARTER), lambda m, at: (m, 0, 0)),
        ),
        compiler_params=params(56),
        cost_estimate=pl.CostEstimate(
            flops=PADDED * WIDTH * SHARE, bytes_accessed=8_000_000, transcendentals=0
        ),
    )(at, *parts, summed, block)


def turn_kernel(*refs):
    half = len(refs) // 3 * 2
    for i, out in enumerate(refs[half:]):
        for c in range(QUARTER // TOK):
            cols = slice(c * TOK, (c + 1) * TOK)
            out[cols, :HALF] = refs[2 * i][:, cols].T
            out[cols, HALF:] = refs[2 * i + 1][:, cols].T


def turn(parts):
    whole = pl.BlockSpec(memory_space=VMEM)
    n = len(parts) // 2
    return pl.pallas_call(
        turn_kernel,
        out_shape=(jax.ShapeDtypeStruct((QUARTER, PADDED), BF16),) * n,
        in_specs=[whole] * (2 * n),
        out_specs=(whole,) * n,
        compiler_params=params(24),
        cost_estimate=pl.CostEstimate(flops=0, bytes_accessed=3_000_000 * n, transcendentals=0),
    )(*parts)


def grads_kernel(at_ref, x0, x1, x2, x3, slope_ref, gg_ref, gu_ref):
    slope = slope_ref[...]
    step = QUARTER // 4
    for rel, x in zip((0, 3, 1, 2), (x0, x1, x2, x3)):
        base = offset(at_ref, rel)

        def body(c, _, x=x, base=base):
            grad = dot(x[pl.ds(pl.multiple_of(c * step, 32), step), :], slope).astype(BF16)
            to = pl.ds(pl.multiple_of(base + c * step, 32), step)
            gg_ref[to, :] = grad[:, :SHARE]
            gu_ref[to, :] = grad[:, SHARE:]
            return 0

        lax.fori_loop(0, 4, body, 0)


def grads(at, xs, slope):
    whole = pl.BlockSpec(memory_space=VMEM)
    return pl.pallas_call(
        grads_kernel,
        out_shape=(jax.ShapeDtypeStruct((WIDTH, SHARE), BF16),) * 2,
        in_specs=[pl.BlockSpec(memory_space=pltpu.SMEM)] + [whole] * 5,
        out_specs=(whole,) * 2,
        compiler_params=params(32),
        cost_estimate=pl.CostEstimate(
            flops=4 * PADDED * WIDTH * SHARE, bytes_accessed=11_000_000, transcendentals=0
        ),
    )(at, *xs, slope)


def down_kernel(h0, h1, h2, h3, rows_ref, *outs):
    rows = rows_ref[...].reshape(PADDED, QUARTER)
    for h, out in zip((h0, h1, h2, h3), outs):
        out[...] = dot(h[...], rows, 0, 0).astype(BF16)


def down_grads(hids, rows):
    whole = pl.BlockSpec(memory_space=VMEM)
    return pl.pallas_call(
        down_kernel,
        out_shape=(jax.ShapeDtypeStruct((SHARE, QUARTER), BF16),) * N_DP,
        in_specs=[whole] * 5,
        out_specs=(whole,) * N_DP,
        compiler_params=params(24),
        cost_estimate=pl.CostEstimate(
            flops=HEAVY, bytes_accessed=5_000_000, transcendentals=0
        ),
    )(*hids, rows)


def join_kernel(slot_ref, here_ref, *refs):
    n = len(refs) // 3
    same = slot_ref[here_ref[0]] == slot_ref[here_ref[0] ^ 1]
    for mine_ref, other_ref, out_ref in zip(refs[:n], refs[n:2 * n], refs[2 * n:]):
        mine = mine_ref[...].astype(F32)
        out_ref[...] = jnp.where(same, mine + other_ref[...].astype(F32), mine).astype(BF16)


def join(slot_expert, here, mine, steps):
    other = [swap(array) for array in mine]
    rows, cols = mine[0].shape
    block = pl.BlockSpec((rows // steps, cols), lambda m, slot, here: (m, 0))
    return pl.pallas_call(
        join_kernel,
        out_shape=(jax.ShapeDtypeStruct((rows, cols), BF16),) * len(mine),
        grid_spec=pltpu.PrefetchScalarGridSpec(
            num_scalar_prefetch=2, grid=(steps,),
            in_specs=[block] * (2 * len(mine)), out_specs=(block,) * len(mine),
        ),
        compiler_params=params(24),
        cost_estimate=pl.CostEstimate(flops=0, bytes_accessed=0, transcendentals=0),
    )(slot_expert, here, *mine, *other)


def place_kernel(at_ref, p0, p1, p2, p3, out_ref):
    for rel, p in enumerate((p0, p1, p2, p3)):
        out_ref[:, pl.ds(offset(at_ref, rel), QUARTER)] = p[...]


def placed(at, parts):
    whole = pl.BlockSpec(memory_space=VMEM)
    return pl.pallas_call(
        place_kernel,
        out_shape=jax.ShapeDtypeStruct((SHARE, WIDTH), BF16),
        in_specs=[pl.BlockSpec(memory_space=pltpu.SMEM)] + [whole] * 4,
        out_specs=whole,
        compiler_params=params(16),
        cost_estimate=pl.CostEstimate(flops=0, bytes_accessed=0, transcendentals=0),
    )(at, *parts)


def shift(x, by):
    return lax.ppermute(x, "dp", [(i, (i + by) % N_DP) for i in range(N_DP)])


def swap(x):
    return lax.ppermute(x, "expert", [(i, i ^ 1) for i in range(SLOTS)])


def exchange(rows):
    return lax.all_to_all(
        rows.reshape(SLOTS, 3, 4, QUARTER), "expert", split_axis=0, concat_axis=0, tiled=True
    ).reshape(FOURS, 4, QUARTER)


def ring(low, high):
    low_below, high_above = shift(low, 1), shift(high, -1)
    high_below, low_above = shift(high, 1), shift(low, -1)
    far = [shift(low_below, 1), shift(high_above, -1)]
    return [low, high], [low_below, high_below], [low_above, high_above], far


def ordered(arrays):
    return lax.optimization_barrier(arrays)


def shards(tokens, cotangent, expert_ids, gate_probs, slot_expert, w_gate, w_up, w_down):
    here = lax.axis_index("expert")
    at = lax.axis_index("dp").reshape(1)
    parity = (here % 2).reshape(1)
    wg, wu, wd = w_gate[0], w_up[0], w_down[0]
    ids, probs = expert_ids.T, gate_probs.T
    slot = jnp.broadcast_to(slot_expert.astype(F32)[:, None], (SLOTS, TOK))
    x_rows, code, pick, scaled = pack(parity, slot, ids, probs, tokens)
    d_rows = scale(scaled, cotangent)
    *sent, few = weights(at, wg, wu, wd)
    x_rows, token = ordered((x_rows, swap(few)))
    sent[1] = ordered((sent[1], x_rows))[0]
    blocks = [shift(w, b) for w, b in zip(sent, (1, 2, 3))]
    x_here = exchange(x_rows)
    x_own, x_below, x_above, x_far = ring(*halves(x_here, token))
    d_here = exchange(d_rows)

    own, *out = terms(at, d_here, wd, blocks)
    others = [shift(out[b - 1], -b) for b in (2, 1, 3)]
    x_parts, own = ordered((x_own + x_below + x_above, own))
    hid, act, ups = forward(at, x_far, near(at, x_parts, wg, wu), wg, wu)
    slope = slopes(own, others, hid, act, ups)
    s_below, s_above = shift(slope, 1), shift(slope, -1)
    x_turned = turn(ordered((x_parts + x_far, slope))[0])
    s_below, s_above, x_turned = ordered((s_below, s_above, x_turned))
    s_far = [shift(s_below[:HALF], 1), shift(s_above[HALF:], -1)]
    s_near = (slope, s_below, s_above)
    s_far, summed = ordered((s_far, back_near(at, s_near, wg, wu, blocks)))
    pay = back_rows(at, (*s_near, *s_far), summed, blocks[1])
    back = exchange(pay)
    d_tokens, d_probs = combine(slot, ids, probs, code, pick, back)

    hid = ordered((hid, s_far))[0]
    pieces = down_grads([hid] + [shift(hid, b) for b in (1, 2, 3)], d_here)
    down = placed(at, [pieces[0]] + [shift(pieces[b], -b) for b in (1, 2, 3)])
    grad_gate, grad_up = join(slot_expert, here.reshape(1), grads(at, x_turned, ordered((slope, pay))[0]), 4)
    grad_down = join(slot_expert, here.reshape(1), [down], 2)[0]
    return d_tokens, d_probs.T, grad_gate[None], grad_up[None], grad_down[None]


def solution(mesh):
    specs = (
        P("expert", "dp"),
        P("expert", "dp"),
        P("expert", None),
        P("expert", None),
        P(),
        P("expert", None, "dp"),
        P("expert", None, "dp"),
        P("expert", "dp", None),
    )
    return jax.shard_map(
        shards,
        mesh=mesh,
        in_specs=specs,
        out_specs=(
            P("expert", "dp"),
            P("expert", None),
            P("expert", None, "dp"),
            P("expert", None, "dp"),
            P("expert", "dp", None),
        ),
        check_vma=False,
    )
```
